256 devices in a mesh: policy: 8 (over x_lo, y), zero: 32 (over x_hi, z, core).
Axes of the slice: x: 4 (x_hi: 2, x_lo: 2; x = x_hi * 2 + x_lo), y: 4, z: 8, core: 2. Of those that a mesh axis runs over, the one named last changes fastest.
Arguments:
- acts: bfloat16 [8, 20480, 4608], P('policy', 'zero'), may hold values from -6 to 6
- cotan: bfloat16 [8, 20480, 1024], P('policy', 'zero'), may hold values from -6 to 6
- advantage: int32 [8, 160], P('policy', 'zero'), may hold values from -4 to 4
- merge_ratio: int32 [8], replicated, may hold values from 1 to 8
- weight: bfloat16 [8, 4608, 1024], P('policy', 'zero'), may hold values from -0.3125 to 0.3125
- anchor: float32 [8, 4608, 1024], P('policy', 'zero'), may hold values from -0.3125 to 0.3125
- init: bfloat16 [4608, 1024], P('zero'), may hold values from -0.62 to 0.62
Outputs:
- anchor_new: float32 [8, 4608, 1024], P('policy', 'zero')
- merged: bfloat16 [4608, 1024], P('zero')
- merged_out: float32 [8, 20480, 1024], P('policy', 'zero')
The draws below stay inside these ranges and needn't reach their ends.
All inputs are finite; a program needn't handle non-finite values.
Results may differ from the reference program's by a relative error of at most 0.015.
Values may be sent and summed in bfloat16 or wider, within the bound.
No kernel may reach another device: no remote copies, remote signals or barrier semaphores. Data moves between devices by JAX's collectives and lax.ppermute only.
A program may use at most 128 MiB of HBM per device.

```python
import math
import jax
import jax.numpy as jnp
from jax import lax

D = 4608
KV = 1024
SEQ = 128
TOK_DEV = 640
POLICIES = 8
TOKENS = 20480
N_ZERO = 32


def draw_init(key, part):
    key = jax.random.fold_in(key, 7)
    first, second = jax.random.split(key)
    rows = jnp.arange(D, dtype=jnp.float32)[:, None]
    base = jnp.clip(jax.random.normal(first, (D, KV), jnp.float32), -5.0, 5.0)
    spread = jnp.exp(jax.random.uniform(second, (D, 1), jnp.float32, 0.0, math.log(4.0)))
    return (0.01 * base * spread * jnp.exp(rows / D * math.log(3.0))).astype(jnp.bfloat16)


def touch_ends(array, own_key, least, high):
    dims = array.shape
    index_at = [jax.random.randint(jax.random.fold_in(own_key, axis), (), 0, dims[axis]) for axis in range(len(dims))]
    array = array.at[tuple(index_at)].set(least)
    longest = dims.index(max(dims))
    index_at[longest] = (index_at[longest] + 1) % dims[longest]
    return array.at[tuple(index_at)].set(high)


def block_levels(key, extent, cuts, low, largest):
    loudness, own = 1.0, jax.random.fold_in(key, 6)
    for position, blocks in cuts:
        heights = jnp.exp(jax.random.uniform(jax.random.fold_in(own, position), (blocks,), jnp.float32, low / len(cuts), largest / len(cuts)))
        loudness = loudness * jnp.repeat(heights, extent[position] // blocks).reshape([-1 if axis == position else 1 for axis in range(len(extent))])
    return loudness


def noise(own_key, extent, scale, most, pieces=(), kind=jnp.bfloat16):
    gain = block_levels(own_key, extent, pieces, -0.22, 0.18) if pieces else 1.0
    array = jax.random.normal(own_key, extent, jnp.float32) * scale * gain
    return jnp.minimum(jnp.maximum(array, -most), most).astype(kind)


def setup_inputs(seed: int = 0) -> dict:
    seeds = jax.random.split(jax.random.key(seed), 8)
    acts = noise(seeds[0], (POLICIES, TOKENS, D), 1.0, 6.0, ((0, 8), (1, 32)))
    cotan = noise(seeds[1], (POLICIES, TOKENS, KV), 1.0, 6.0, ((0, 8), (1, 32)))
    advantage = touch_ends(jax.random.randint(seeds[2], (POLICIES, TOKENS // SEQ), -4, 5), jax.random.fold_in(seeds[2], 1), -4, 4).astype(jnp.int32)
    merge_ratio = touch_ends(jax.random.randint(seeds[3], (POLICIES,), 1, 9), jax.random.fold_in(seeds[3], 1), 1, 8).astype(jnp.int32)
    weight = noise(seeds[4], (POLICIES, D, KV), 0.02, 0.3125, ((0, 8), (1, 32)))
    anchor = noise(seeds[5], (POLICIES, D, KV), 0.02, 0.3125, ((0, 8), (1, 32)), jnp.float32)
    init = draw_init(jax.random.fold_in(seeds[7], 71), 0)
    return {"acts": acts, "cotan": cotan, "advantage": advantage, "merge_ratio": merge_ratio, "weight": weight, "anchor": anchor, "init": init}


step_size = 0.02
ema_decay = 0.9

def reference(acts, cotan, advantage, merge_ratio, weight, anchor, init):
    tokens = acts.shape[1]
    ratio = merge_ratio.astype(jnp.float32)
    share = ratio / jnp.sum(ratio)
    init_wide = init.astype(jnp.float32)
    anchors = []
    target = jnp.float32(0.0)
    mixed = jnp.zeros(init.shape, jnp.float32)
    for policy_idx in range(POLICIES):
        levels = jnp.repeat(advantage[policy_idx].astype(jnp.float32) * 0.25, SEQ)
        scaled = (cotan[policy_idx].astype(jnp.float32) * levels[:, None]).astype(jnp.bfloat16)
        act_blocks = acts[policy_idx].reshape(N_ZERO, TOK_DEV, D)
        scaled_blocks = scaled.reshape(N_ZERO, TOK_DEV, KV)

        def add_block(total, pair):
            block_acts, block_scaled = pair
            term = lax.dot_general(block_acts, block_scaled, (((0,), (0,)), ((), ())), preferred_element_type=jnp.float32)
            return (total + term.astype(jnp.bfloat16).astype(jnp.float32), None)
        grad, unused = lax.scan(add_block, jnp.zeros((D, KV), jnp.float32), (act_blocks, scaled_blocks))
        updated = weight[policy_idx].astype(jnp.float32) - step_size * grad / math.sqrt(tokens)
        anchors.append(ema_decay * anchor[policy_idx] + (1.0 - ema_decay) * updated)
        task = updated - init_wide
        target = target + share[policy_idx] * jnp.sqrt(jnp.sum(task * task))
        mixed = mixed + share[policy_idx] * task
    mixed_sq = jnp.sum(mixed * mixed)
    merged = (init_wide + mixed * (target / jnp.sqrt(mixed_sq))).astype(jnp.bfloat16)
    outputs = []
    for policy_idx in range(POLICIES):
        outputs.append(jnp.dot(acts[policy_idx], merged, preferred_element_type=jnp.float32))
    return (jnp.stack(anchors), merged, jnp.stack(outputs))
```

```python
import functools
import math

import jax
import jax.numpy as jnp
from jax import lax
from jax.experimental import pallas as pl
from jax.experimental.pallas import tpu as pltpu
from jax.sharding import Mesh, PartitionSpec as P

SEQ = 128
step_size = 0.02
ema_decay = 0.9

XL, NY, XH, NZ, NC = 2, 4, 2, 8, 2
F32, BF16 = jnp.float32, jnp.bfloat16

COLS_A = 384
VMEM_LIMIT = 56 * 1024 * 1024


def swap(a, axis, bit=1):
    size = {"xl": XL, "y": NY, "xh": XH, "z": NZ, "c": NC}[axis]
    return lax.ppermute(a, axis, [(i, i ^ bit) for i in range(size)])


def shift(a, by):
    return lax.ppermute(a, "z", [(i, (i + by) % NZ) for i in range(NZ)])


def after(a, *others):
    return lax.optimization_barrier((a, others))[0]


def tie(*arrays):
    return lax.optimization_barrier(arrays)


def grad_kernel(where_ref, level_ref, acts_ref, cotan_ref, own_ref, other_ref, scaled_ref):
    half = own_ref.shape[-1]

    @pl.when(pl.program_id(0) == 0)
    def _():
        first = where_ref[0] == 0
        for seq in range(level_ref.shape[0]):
            rows = pl.ds(seq * SEQ, SEQ)
            level = level_ref[seq].astype(F32) * 0.25
            low, high = cotan_ref[rows, :half], cotan_ref[rows, half:]
            scaled_ref[rows, :half] = (jnp.where(first, low, high).astype(F32) * level).astype(BF16)
            scaled_ref[rows, half:] = (jnp.where(first, high, low).astype(F32) * level).astype(BF16)

    out = lax.dot_general(
        acts_ref[...], scaled_ref[...], (((0,), (0,)), ((), ())), preferred_element_type=F32
    ).astype(BF16)
    own_ref[...] = out[:, :half].reshape(own_ref.shape)
    other_ref[...] = out[:, half:].reshape(other_ref.shape)


def partial_grad(core, side, levels, acts, cotan):
    tokens, width = acts.shape
    kv = cotan.shape[1]
    rows = width // (XH * NZ)
    steps = 2
    out = jax.ShapeDtypeStruct((NZ, rows, kv // 2), BF16)
    spec = pl.BlockSpec((NZ // steps, rows, kv // 2), lambda i, *_: (i, 0, 0))
    return pl.pallas_call(
        grad_kernel,
        grid_spec=pltpu.PrefetchScalarGridSpec(
            num_scalar_prefetch=2,
            grid=(steps,),
            in_specs=[
                pl.BlockSpec((tokens, width // (XH * steps)), lambda i, at, _: (0, at[1] * steps + i)),
                pl.BlockSpec((tokens, kv), lambda i, *_: (0, 0)),
            ],
            out_specs=[spec, spec],
            scratch_shapes=[pltpu.VMEM((tokens, kv), BF16)],
        ),
        out_shape=[out, out],
        compiler_params=pltpu.CompilerParams(vmem_limit_bytes=VMEM_LIMIT),
        cost_estimate=pl.CostEstimate(
            flops=tokens * width * kv,
            bytes_accessed=tokens * width + 2 * tokens * kv + width * kv,
            transcendentals=0,
        ),
        name="partial_grad",
    )(jnp.stack([core, side]).astype(jnp.int32), levels, acts, cotan)


def out_kernel(where_ref, own_ref, other_ref, *refs, slots):
    chunks, (out_own, out_other, whole, sems) = refs[: len(slots)], refs[len(slots) :]
    rows = whole.shape[0] // (XH * NZ)

    @pl.when(pl.program_id(0) == 0)
    def _():
        copies = []
        index = 0
        for ref, places in zip(chunks, slots):
            for place, (src, row, size) in enumerate(places):
                at = where_ref[index] * rows + row
                copies.append(
                    pltpu.make_async_copy(
                        ref.at[src] if src is not None else ref,
                        whole.at[pl.ds(pl.multiple_of(at, 16), size)],
                        sems.at[index],
                    )
                )
                index += 1
        for copy in copies:
            copy.start()
        for copy in copies:
            copy.wait()

    out_own[...] = jnp.dot(own_ref[...], whole[...], preferred_element_type=F32)
    out_other[...] = jnp.dot(other_ref[...], whole[...], preferred_element_type=F32)


def project(acts, acts_other, chunks, slots, where):
    tokens, width = acts.shape
    cols = chunks[0].shape[-1]
    steps = 4
    count = sum(len(s) for s in slots)
    out = jax.ShapeDtypeStruct((tokens, cols), F32)
    a_spec = pl.BlockSpec((tokens // steps, width), lambda i, *_: (i, 0))
    o_spec = pl.BlockSpec((tokens // steps, cols), lambda i, *_: (i, 0))
    return pl.pallas_call(
        functools.partial(out_kernel, slots=slots),
        grid_spec=pltpu.PrefetchScalarGridSpec(
            num_scalar_prefetch=1,
            grid=(steps,),
            in_specs=[a_spec, a_spec] + [pl.BlockSpec(memory_space=pl.ANY)] * len(chunks),
            out_specs=[o_spec, o_spec],
            scratch_shapes=[pltpu.VMEM((width, cols), BF16), pltpu.SemaphoreType.DMA((count,))],
        ),
        out_shape=[out, out],
        compiler_params=pltpu.CompilerParams(vmem_limit_bytes=VMEM_LIMIT),
        cost_estimate=pl.CostEstimate(
            flops=4 * tokens * width * cols,
            bytes_accessed=4 * tokens * width + 2 * width * cols + 8 * tokens * cols,
            transcendentals=0,
        ),
        name="project",
    )(where, acts, acts_other, *chunks)


def on_device(acts, cotan, advantage, merge_ratio, weight, anchor, init):
    acts, cotan, levels, weight, anchor = acts[0], cotan[0], advantage[0], weight[0], anchor[0]
    tokens, width = acts.shape
    kv = cotan.shape[1]
    half = kv // 2
    blocks = XH * NZ
    own_rows = width // (blocks * NC)
    rows = own_rows * NC
    cols_a = COLS_A
    total_tokens = tokens * blocks * NC
    core, z, xh = lax.axis_index("c"), lax.axis_index("z"), lax.axis_index("xh")
    policy = lax.axis_index("xl") * NY + lax.axis_index("y")

    def my_half(a):
        return lax.dynamic_slice_in_dim(a, core * half, half, axis=-1)

    def other_half(a):
        return lax.dynamic_slice_in_dim(a, (1 - core) * half, half, axis=-1)

    def both_rows(mine, theirs):
        return jnp.where(core == 0, jnp.concatenate([mine, theirs], -2), jnp.concatenate([theirs, mine], -2))

    def both_cols(mine, theirs):
        return jnp.where(core == 0, jnp.concatenate([mine, theirs], -1), jnp.concatenate([theirs, mine], -1))

    given = jnp.stack([weight, init])
    given_got = swap(other_half(given), "c")
    given = both_rows(my_half(given), given_got).astype(F32)
    weight_half, init_half = given[0], given[1]

    far_own, far_other = partial_grad(core, 1 - xh, levels, acts, cotan)
    far_got = swap(far_other, "c")
    near_own, near_other = partial_grad(core, xh, levels, after(acts, far_own, given_got), cotan)
    near_got = swap(near_other, "c")
    acts_other = swap(after(acts, near_got), "c")

    def pick(a, k, at=0, cols=0):
        cols = cols or a.shape[-1]
        return lax.dynamic_slice(a, ((z + k + NZ) % NZ, 0, at), (1, rows, cols))[0].astype(F32)

    sent_b = (far_own[..., cols_a:].astype(F32) + far_got[..., cols_a:].astype(F32)).astype(BF16)
    back_b = swap(sent_b, "xh")

    def term_a(k, own, got):
        return pick(own, k, 0, cols_a) + pick(got, k, 0, cols_a)

    def far(k):
        return term_a(k, far_own, far_got)

    def near(k):
        return term_a(k, near_own, near_got)

    def pair(first, second):
        return jnp.stack([first.astype(BF16), second.astype(BF16)])

    down = shift(after(far(-4).astype(BF16), sent_b), -1)
    up = shift(near(4).astype(BF16), 1)
    down, up = tie(down, up)
    cut = rows // 2
    send_down = pair(far(-3) + down.astype(F32), near(-3))
    send_up = pair(far(3), near(3) + up.astype(F32))
    down, up = tie(shift(send_down, -1), shift(send_up, 1))
    held_b = after(back_b, send_down, send_up, acts_other)

    def term_b(k):
        return pick(near_own, k, cols_a, half - cols_a) + pick(near_got, k, cols_a, half - cols_a) + pick(held_b, k)

    down_b = shift(term_b(-4)[:cut].astype(BF16), -1)
    up_b = shift(term_b(4)[cut:].astype(BF16), 1)
    send_down = pair(far(-2) + down[0].astype(F32), near(-2) + down[1].astype(F32))
    send_up = pair(far(2) + up[0].astype(F32), near(2) + up[1].astype(F32))
    down, up = tie(shift(send_down, -1), shift(send_up, 1))
    down_b, up_b = after(down_b, send_down, send_up), after(up_b, send_down, send_up)
    t = term_b(-3)
    down_b = shift(jnp.concatenate([t[:cut] + down_b.astype(F32), t[cut:]]).astype(BF16), -1)
    t = term_b(3)
    up_b = shift(jnp.concatenate([t[:cut], t[cut:] + up_b.astype(F32)]).astype(BF16), 1)
    send_down = pair(far(-1) + down[0].astype(F32), near(-1) + down[1].astype(F32))
    send_up = pair(far(1) + up[0].astype(F32), near(1) + up[1].astype(F32))
    down, up = tie(shift(send_down, -1), shift(send_up, 1))
    down_b, up_b = after(down_b, send_down, send_up), after(up_b, send_down, send_up)
    down_b = shift((term_b(-2) + down_b.astype(F32)).astype(BF16), -1)
    up_b = shift((term_b(2) + up_b.astype(F32)).astype(BF16), 1)
    sent_a = (far(0) + down[0].astype(F32) + up[0].astype(F32)).astype(BF16)
    back_a = swap(sent_a, "xh")
    down_b, up_b = after(down_b, sent_a), after(up_b, sent_a)
    down_b = shift((term_b(-1) + down_b.astype(F32)).astype(BF16), -1)
    up_b = shift((term_b(1) + up_b.astype(F32)).astype(BF16), 1)
    grad_a = near(0) + down[1].astype(F32) + up[1].astype(F32) + back_a.astype(F32)
    grad_b = term_b(0) + down_b.astype(F32) + up_b.astype(F32)
    grad = jnp.concatenate([grad_a, grad_b], axis=1)

    updated = weight_half - step_size * grad / math.sqrt(total_tokens)
    task = updated - init_half
    ratio = merge_ratio.astype(F32)
    shares = ratio / jnp.sum(ratio)
    norm = jnp.sum(task * task)
    norms = jnp.where(lax.broadcasted_iota(jnp.int32, (8, 128), 0) == policy, norm, 0.0)
    mix = (shares[policy] * updated).astype(BF16)
    for axis, bit in (("xl", 1), ("y", 1), ("y", 2)):
        norms, mix = lax.optimization_barrier((norms, mix))
        norms_got, mix_got = lax.optimization_barrier((swap(norms, axis, bit), swap(mix, axis, bit)))
        norms = norms + norms_got
        mix = mix.astype(F32) + mix_got.astype(F32)
        if (axis, bit) != ("y", 2):
            mix = mix.astype(BF16)
    mixed = mix - init_half
    mixed_sq = jnp.sum(mixed * mixed)
    scalars = jnp.where(lax.broadcasted_iota(jnp.int32, (8, 128), 1) == 0, norms, mixed_sq)
    for axis, bit in (("c", 1), ("xh", 1), ("z", 1), ("z", 2), ("z", 4)):
        scalars = scalars + swap(scalars, axis, bit)
    target = jnp.sum(shares * jnp.sqrt(scalars[:, 0]))
    merged = (init_half + mixed * (target / jnp.sqrt(scalars[0, 1]))).astype(BF16)

    merged_a, block_b = merged[:, :cols_a], merged[:, cols_a:]
    x_pair = jnp.stack([merged_a, swap(merged_a, "xh")])
    held = after(block_b, merged_a)
    ups_b, downs_b = [shift(held, 1)], [shift(held, -1)]
    ups_a, downs_a = [shift(x_pair, 1)], [shift(x_pair, -1)]
    last = x_pair
    for k in (2, 3):
        ups_b.append(shift(after(ups_b[-1], last), 1))
        downs_b.append(shift(after(downs_b[-1], last), -1))
        last = (ups_a[-1], downs_a[-1])
        ups_a.append(shift(ups_a[-1], 1))
        downs_a.append(shift(downs_a[-1], -1))
    up_b = shift(after(ups_b[-1], last)[:cut], 1)
    down_b = shift(after(downs_b[-1], last)[cut:], -1)
    up_a = shift(ups_a[-1][:, :cut], 1)
    down_a = shift(downs_a[-1][:, cut:], -1)
    stack = jnp.stack([block_b, *ups_b, *downs_b, jnp.concatenate([up_b, down_b])])
    across = swap(stack, "xh")
    order = [0, -1, -2, -3, 1, 2, 3, 4]

    def place(x, k):
        return (x * NZ + (z + k + NZ) % NZ).astype(jnp.int32)

    slots_b = [[(i, 0, rows) for i in range(NZ)]] * 2
    where_b = jnp.stack([place(xh, k) for k in order] + [place(1 - xh, k) for k in order])
    chunks_a = [x_pair, *ups_a, *downs_a, up_a, down_a]
    slots_a = [[(0, 0, rows), (1, 0, rows)]] * (NZ - 1) + [
        [(0, 0, cut), (1, 0, cut)],
        [(0, cut, rows - cut), (1, cut, rows - cut)],
    ]
    where_a = jnp.stack([place(x, k) for k in order + [4] for x in (xh, 1 - xh)])

    out_b, away_b = project(after(acts, ups_a[-1], downs_a[-1]), acts_other, [stack, across], slots_b, where_b)
    home_b = swap(away_b, "c")
    out_a, away_a = project(after(acts, out_b), acts_other, chunks_a, slots_a, where_a)
    home_a = swap(away_a, "c")
    result = both_cols(jnp.concatenate([out_a, out_b], 1), jnp.concatenate([home_a, home_b], 1))

    def to_rows(a):
        mine = lax.dynamic_slice_in_dim(a, core * own_rows, own_rows, axis=0)
        theirs = lax.dynamic_slice_in_dim(a, (1 - core) * own_rows, own_rows, axis=0)
        return both_cols(mine, swap(theirs, "c"))

    grad_rows = to_rows(grad.astype(BF16)).astype(F32)
    anchor_new = ema_decay * anchor + (1.0 - ema_decay) * (
        weight.astype(F32) - step_size * grad_rows / math.sqrt(total_tokens)
    )
    return anchor_new[None], to_rows(merged), result[None]


def solution(mesh):
    mesh = Mesh(mesh.devices.reshape(XL, NY, XH, NZ, NC), ("xl", "y", "xh", "z", "c"))
    policy, zero = ("xl", "y"), ("xh", "z", "c")
    placed = (
        P(policy, zero, None),
        P(policy, zero, None),
        P(policy, zero),
        P(),
        P(policy, zero, None),
        P(policy, zero, None),
        P(zero, None),
    )
    return jax.shard_map(
        on_device,
        mesh=mesh,
        in_specs=placed,
        out_specs=(P(policy, zero, None), P(zero, None), P(policy, zero, None)),
        check_vma=False,
    )
```

```python
import functools
import math

import jax
import jax.numpy as jnp
from jax import lax
from jax.experimental import pallas as pl
from jax.experimental.pallas import tpu as pltpu
from jax.sharding import Mesh, PartitionSpec as P

SEQ = 128
step_size = 0.02
ema_decay = 0.9

XL, NY, XH, NZ, NC = 2, 4, 2, 8, 2
F32, BF16 = jnp.float32, jnp.bfloat16

COLS_A = 256
VMEM_LIMIT = 56 * 1024 * 1024


def swap(a, axis, bit=1):
    size = {"xl": XL, "y": NY, "xh": XH, "z": NZ, "c": NC}[axis]
    return lax.ppermute(a, axis, [(i, i ^ bit) for i in range(size)])


def shift(a, by):
    return lax.ppermute(a, "z", [(i, (i + by) % NZ) for i in range(NZ)])


def after(a, *others):
    return lax.optimization_barrier((a, others))[0]


def tie(*arrays):
    return lax.optimization_barrier(arrays)


def grad_kernel(where_ref, level_ref, acts_ref, cotan_ref, *refs):
    outs, scaled_ref = refs[:4], refs[4]
    half = scaled_ref.shape[1] // 2

    @pl.when(pl.program_id(0) == 0)
    def _():
        first = where_ref[0] == 0
        for seq in range(level_ref.shape[0]):
            rows = pl.ds(seq * SEQ, SEQ)
            level = level_ref[seq].astype(F32) * 0.25
            low, high = cotan_ref[rows, :half], cotan_ref[rows, half:]
            scaled_ref[rows, :half] = (jnp.where(first, low, high).astype(F32) * level).astype(BF16)
            scaled_ref[rows, half:] = (jnp.where(first, high, low).astype(F32) * level).astype(BF16)

    product = lax.dot_general(
        acts_ref[...], scaled_ref[...], (((0,), (0,)), ((), ())), preferred_element_type=F32
    ).astype(BF16)
    at = 0
    for out in outs:
        cols = out.shape[-1]
        out[...] = product[:, at : at + cols].reshape(out.shape)
        at += cols


def partial_grad(core, side, levels, acts, cotan):
    tokens, width = acts.shape
    kv = cotan.shape[1]
    rows = width // (XH * NZ)
    steps = 2
    outs, specs = [], []
    for cols in (COLS_A, kv // 2 - COLS_A) * 2:
        outs.append(jax.ShapeDtypeStruct((XH, NZ, rows, cols), BF16))
        specs.append(pl.BlockSpec((1, NZ // steps, rows, cols), lambda i, *_: (i // steps, i % steps, 0, 0)))

    def block(i, at, _):
        return 0, jnp.where(i < steps, 1 - at[1], at[1]) * steps + i % steps

    return pl.pallas_call(
        grad_kernel,
        grid_spec=pltpu.PrefetchScalarGridSpec(
            num_scalar_prefetch=2,
            grid=(XH * steps,),
            in_specs=[
                pl.BlockSpec((tokens, width // (XH * steps)), block),
                pl.BlockSpec((tokens, kv), lambda i, *_: (0, 0)),
            ],
            out_specs=specs,
            scratch_shapes=[pltpu.VMEM((tokens, kv), BF16)],
        ),
        out_shape=outs,
        compiler_params=pltpu.CompilerParams(vmem_limit_bytes=VMEM_LIMIT),
        cost_estimate=pl.CostEstimate(
            flops=2 * tokens * width * kv,
            bytes_accessed=2 * (tokens * width + tokens * kv + width * kv),
            transcendentals=0,
        ),
        name="partial_grad",
    )(jnp.stack([core, side]).astype(jnp.int32), levels, acts, cotan)


def out_kernel(where_ref, own_ref, other_ref, *refs, slots):
    chunks, (out_own, out_other, whole, sems) = refs[: len(slots)], refs[len(slots) :]
    rows = whole.shape[0] // (XH * NZ)
    step = pl.program_id(0)
    depth = own_ref.shape[1]

    @pl.when(step == 0)
    def _():
        copies = []
        for ref, (col, places) in zip(chunks, slots):
            for src, row, size in places:
                index = len(copies)
                at = where_ref[index] * rows + row
                copies.append(
                    pltpu.make_async_copy(
                        ref.at[src],
                        whole.at[pl.ds(pl.multiple_of(at, 16), size), pl.ds(col, ref.shape[-1])],
                        sems.at[index],
                    )
                )
        for copy in copies:
            copy.start()
        for copy in copies:
            copy.wait()
        out_own[...] = jnp.zeros_like(out_own)
        out_other[...] = jnp.zeros_like(out_other)

    merged = whole[pl.ds(pl.multiple_of(step * depth, depth), depth), :]
    out_other[...] += jnp.dot(other_ref[...], merged, preferred_element_type=F32)
    out_own[...] += jnp.dot(own_ref[...], merged, preferred_element_type=F32)


def project(acts, acts_other, chunks, slots, where, cols):
    tokens, width = acts.shape
    steps = 4
    out = jax.ShapeDtypeStruct((tokens, cols), F32)
    a_spec = pl.BlockSpec((tokens, width // steps), lambda i, *_: (0, i))
    o_spec = pl.BlockSpec((tokens, cols), lambda i, *_: (0, 0))
    return pl.pallas_call(
        functools.partial(out_kernel, slots=slots),
        grid_spec=pltpu.PrefetchScalarGridSpec(
            num_scalar_prefetch=1,
            grid=(steps,),
            in_specs=[a_spec, a_spec] + [pl.BlockSpec(memory_space=pl.ANY)] * len(chunks),
            out_specs=[o_spec, o_spec],
            scratch_shapes=[pltpu.VMEM((width, cols), BF16), pltpu.SemaphoreType.DMA((where.shape[0],))],
        ),
        out_shape=[out, out],
        compiler_params=pltpu.CompilerParams(vmem_limit_bytes=VMEM_LIMIT),
        cost_estimate=pl.CostEstimate(
            flops=4 * tokens * width * cols,
            bytes_accessed=4 * tokens * width + 2 * width * cols + 8 * tokens * cols,
            transcendentals=0,
        ),
        name="project",
    )(where, acts, acts_other, *chunks)


def on_device(acts, cotan, advantage, merge_ratio, weight, anchor, init):
    acts, cotan, levels, weight, anchor = acts[0], cotan[0], advantage[0], weight[0], anchor[0]
    tokens, width = acts.shape
    kv = cotan.shape[1]
    half = kv // 2
    blocks = XH * NZ
    own_rows = width // (blocks * NC)
    rows = own_rows * NC
    total_tokens = tokens * blocks * NC
    core, z, xh = lax.axis_index("c"), lax.axis_index("z"), lax.axis_index("xh")
    policy = lax.axis_index("xl") * NY + lax.axis_index("y")

    def my_half(a):
        return lax.dynamic_slice_in_dim(a, core * half, half, axis=-1)

    def other_half(a):
        return lax.dynamic_slice_in_dim(a, (1 - core) * half, half, axis=-1)

    def both_rows(mine, theirs):
        return jnp.where(core == 0, jnp.concatenate([mine, theirs], -2), jnp.concatenate([theirs, mine], -2))

    def both_cols(mine, theirs):
        return jnp.where(core == 0, jnp.concatenate([mine, theirs], -1), jnp.concatenate([theirs, mine], -1))

    given = jnp.stack([weight, init])
    given_got = swap(other_half(given), "c")
    acts_other = swap(acts, "c")
    given = both_rows(my_half(given), given_got)
    weight_half, init_half = given[0].astype(F32), given[1].astype(F32)
    init_pair = jnp.stack([given[1], swap(given[1], "xh")])
    init_up, init_down = shift(init_pair, 1), shift(init_pair, -1)

    *own, other_a, other_b = partial_grad(core, xh, levels, acts, cotan)
    got = [swap(after(other_a, acts_other, init_pair), "c"), swap(after(other_b, acts_other, init_pair), "c")]
    streams = (0, 1)

    def pick(a, k, side, sides):
        cut = lax.dynamic_slice(a, (side, (z + k + NZ) % NZ, 0, 0), (sides, 1, rows, a.shape[-1]))
        return cut.reshape(sides, rows, -1).astype(F32)

    def term(s, k, side=0, sides=2):
        return pick(own[s], k, side, sides) + pick(got[s], k, side, sides)

    zero = ((0, 0), (0, 0))
    cut = rows // 2
    down, up, sums = [None, None], [None, None], [None, None]
    last = ()
    for k in (4, 3, 2, 1, 0):
        for s in streams:
            if k == 4:
                send_down, send_up = term(s, -4, 0, 1), term(s, 4, 1, 1)
                if s == 1:
                    send_down, send_up, *_ = tie(send_down, send_up, init_up, init_down, *last)
            else:
                down[s], up[s], *_ = tie(down[s], up[s], *last)
                from_up, from_down = down[s].astype(F32), up[s].astype(F32)
                if k == 3:
                    from_up = jnp.pad(from_up, ((0, 1), *zero))
                    from_down = jnp.pad(from_down, ((1, 0), *zero))
                if k == 0:
                    sums[s] = term(s, 0) + from_up + from_down
                    send_down = send_up = sums[s][0].astype(BF16)
                else:
                    send_down, send_up = term(s, -k) + from_up, term(s, k) + from_down
            send_down, send_up = send_down.astype(BF16), send_up.astype(BF16)
            last = (send_down, send_up)
            if k == 0:
                down[s] = swap(send_down, "xh")
            else:
                down[s], up[s] = shift(send_down, -1), shift(send_up, 1)

    ratio = merge_ratio.astype(F32)
    shares = ratio / jnp.sum(ratio)
    share = shares[policy]
    bounds = ((0, COLS_A), (COLS_A, half))
    grads, mixes, norm = [None, None], [None, None], 0.0
    for s in streams:
        low, high = bounds[s]
        grads[s] = sums[s][1] + down[s].astype(F32)
        updated = weight_half[:, low:high] - step_size * grads[s] / math.sqrt(total_tokens)
        task = updated - init_half[:, low:high]
        norm = norm + jnp.sum(task * task)
        mixes[s] = (share * updated).astype(BF16)
    norms = jnp.where(lax.broadcasted_iota(jnp.int32, (8, 128), 0) == policy, norm, 0.0)
    last = ()
    for axis, bit in (("xl", 1), ("y", 1), ("y", 2)):
        arrived = [swap(mixes[0], axis, bit), swap(mixes[1], axis, bit)]
        norms_got = swap(after(norms, mixes[1]), axis, bit)
        for s in streams:
            if s == 1:
                arrived[s], norms_got, *_ = tie(arrived[s], norms_got, mixes[0])
                norms = norms + norms_got
            mixes[s] = mixes[s].astype(F32) + arrived[s].astype(F32)
            if (axis, bit) != ("y", 2):
                mixes[s] = mixes[s].astype(BF16)
    mixed_sq = 0.0
    for s in streams:
        low, high = bounds[s]
        mixed = mixes[s] - init_half[:, low:high]
        mixed_sq = mixed_sq + jnp.sum(mixed * mixed)
    scalars = jnp.where(lax.broadcasted_iota(jnp.int32, (8, 128), 1) == 0, norms, mixed_sq)

    def add_over(scalars, axis, bit, *others):
        scalars = after(scalars, *others)
        return scalars + swap(scalars, axis, bit)

    blocks_sent = [m.astype(BF16) for m in mixes]
    across = [swap(a, "xh") for a in blocks_sent]
    scalars = add_over(scalars, "c", 1, *blocks_sent)
    scalars = add_over(scalars, "xh", 1)
    pairs = [jnp.stack([a, b]) for a, b in zip(blocks_sent, across)]
    up, down = [shift(pairs[0], 1), None], [shift(pairs[0], -1), None]
    pairs[1], scalars, _ = tie(pairs[1], scalars, pairs[0])
    up[1], down[1] = shift(pairs[1], 1), shift(pairs[1], -1)
    scalars = add_over(scalars, "z", 1, pairs[1])
    scalars = add_over(scalars, "z", 2)
    scalars = add_over(scalars, "z", 4)
    target = jnp.sum(shares * jnp.sqrt(scalars[:, 0]))
    factor = target / jnp.sqrt(scalars[0, 1])

    def merge(base, mix, s):
        low, high = bounds[s]
        base = base[..., low:high].astype(F32)
        return (base + (mix.astype(F32) - base) * factor).astype(BF16)

    chunks = [[], []]
    last = ()
    for k in (2, 3, 4):
        for s in streams:
            up[s], down[s], *_ = tie(up[s], down[s], *last)
            if k == 2:
                up[s], down[s] = merge(init_up, up[s], s), merge(init_down, down[s], s)
            last = (up[s], down[s])
            chunks[s] += [(up[s], 1 - k), (down[s], k - 1)]
            if k == 4:
                up[s], down[s] = up[s][:, :cut], down[s][:, cut:]
            up[s], down[s] = shift(up[s], 1), shift(down[s], -1)

    def place(x, k):
        return (x * NZ + (z + k + NZ) % NZ).astype(jnp.int32)

    arrays, slots, where, merged = [], [], [], []
    for s in streams:
        mine = merge(init_pair, pairs[s], s)
        merged.append(mine[0])
        for array, k in [(mine, 0)] + chunks[s]:
            arrays.append(array)
            slots.append((bounds[s][0], [(0, 0, rows), (1, 0, rows)]))
            where += [place(xh, k), place(1 - xh, k)]
        for array, row, size in ((up[s], 0, cut), (down[s], cut, rows - cut)):
            arrays.append(array)
            slots.append((bounds[s][0], [(0, row, size), (1, row, size)]))
            where += [place(xh, 4), place(1 - xh, 4)]
    mine, away = project(acts, acts_other, arrays, slots, jnp.stack(where), half)
    result = both_cols(mine, swap(away, "c"))
    merged = jnp.concatenate(merged, axis=1)
    grad = jnp.concatenate(grads, axis=1)

    def to_rows(a):
        mine = lax.dynamic_slice_in_dim(a, core * own_rows, own_rows, axis=0)
        theirs = lax.dynamic_slice_in_dim(a, (1 - core) * own_rows, own_rows, axis=0)
        return both_cols(mine, swap(theirs, "c"))

    grad_rows = to_rows(grad.astype(BF16)).astype(F32)
    anchor_new = ema_decay * anchor + (1.0 - ema_decay) * (
        weight.astype(F32) - step_size * grad_rows / math.sqrt(total_tokens)
    )
    return anchor_new[None], to_rows(merged), result[None]


def solution(mesh):
    mesh = Mesh(mesh.devices.reshape(XL, NY, XH, NZ, NC), ("xl", "y", "xh", "z", "c"))
    policy, zero = ("xl", "y"), ("xh", "z", "c")
    placed = (
        P(policy, zero, None),
        P(policy, zero, None),
        P(policy, zero),
        P(),
        P(policy, zero, None),
        P(policy, zero, None),
        P(zero, None),
    )
    return jax.shard_map(
        on_device,
        mesh=mesh,
        in_specs=placed,
        out_specs=(P(policy, zero, None), P(zero, None), P(policy, zero, None)),
        check_vma=False,
    )
```

```python
import functools
import math

import jax
import jax.numpy as jnp
from jax import lax
from jax.experimental import pallas as pl
from jax.experimental.pallas import tpu as pltpu
from jax.sharding import Mesh, PartitionSpec as P

SEQ = 128
step_size = 0.02
ema_decay = 0.9

XL, NY, XH, NZ, NC = 2, 4, 2, 8, 2
F32, BF16 = jnp.float32, jnp.bfloat16

COLS_A = 256
VMEM_LIMIT = 56 * 1024 * 1024


def swap(a, axis, bit=1):
    size = {"xl": XL, "y": NY, "xh": XH, "z": NZ, "c": NC}[axis]
    return lax.ppermute(a, axis, [(i, i ^ bit) for i in range(size)])


def shift(a, by):
    return lax.ppermute(a, "z", [(i, (i + by) % NZ) for i in range(NZ)])


def after(a, *others):
    return lax.optimization_barrier((a, others))[0]


def tie(*arrays):
    return lax.optimization_barrier(arrays)


def grad_kernel(where_ref, level_ref, acts_ref, cotan_ref, *refs):
    outs, scaled_ref = refs[:4], refs[4]
    half = scaled_ref.shape[1] // 2

    @pl.when(pl.program_id(0) == 0)
    def _():
        first = where_ref[0] == 0
        for seq in range(level_ref.shape[0]):
            rows = pl.ds(seq * SEQ, SEQ)
            level = level_ref[seq].astype(F32) * 0.25
            low, high = cotan_ref[rows, :half], cotan_ref[rows, half:]
            scaled_ref[rows, :half] = (jnp.where(first, low, high).astype(F32) * level).astype(BF16)
            scaled_ref[rows, half:] = (jnp.where(first, high, low).astype(F32) * level).astype(BF16)

    product = lax.dot_general(
        acts_ref[...], scaled_ref[...], (((0,), (0,)), ((), ())), preferred_element_type=F32
    ).astype(BF16)
    at = 0
    for out in outs:
        cols = out.shape[-1]
        out[...] = product[:, at : at + cols].reshape(out.shape)
        at += cols


def partial_grad(core, side, levels, acts, cotan):
    tokens, width = acts.shape
    kv = cotan.shape[1]
    rows = width // (XH * NZ)
    steps = 2
    outs, specs = [], []
    for cols in (COLS_A, kv // 2 - COLS_A) * 2:
        outs.append(jax.ShapeDtypeStruct((XH, NZ, rows, cols), BF16))
        specs.append(pl.BlockSpec((1, NZ // steps, rows, cols), lambda i, *_: (i // steps, i % steps, 0, 0)))

    def block(i, at, _):
        return 0, jnp.where(i < steps, 1 - at[1], at[1]) * steps + i % steps

    return pl.pallas_call(
        grad_kernel,
        grid_spec=pltpu.PrefetchScalarGridSpec(
            num_scalar_prefetch=2,
            grid=(XH * steps,),
            in_specs=[
                pl.BlockSpec((tokens, width // (XH * steps)), block),
                pl.BlockSpec((tokens, kv), lambda i, *_: (0, 0)),
            ],
            out_specs=specs,
            scratch_shapes=[pltpu.VMEM((tokens, kv), BF16)],
        ),
        out_shape=outs,
        compiler_params=pltpu.CompilerParams(vmem_limit_bytes=VMEM_LIMIT),
        cost_estimate=pl.CostEstimate(
            flops=2 * tokens * width * kv,
            bytes_accessed=2 * (tokens * width + tokens * kv + width * kv),
            transcendentals=0,
        ),
        name="partial_grad",
    )(jnp.stack([core, side]).astype(jnp.int32), levels, acts, cotan)


def out_kernel(where_ref, own_ref, other_ref, *refs, slots):
    chunks, (out_own, out_other, whole, sems) = refs[: len(slots)], refs[len(slots) :]
    rows = whole.shape[0] // (XH * NZ)
    step = pl.program_id(0)
    depth = own_ref.shape[1]

    @pl.when(step == 0)
    def _():
        copies = []
        for ref, (col, places) in zip(chunks, slots):
            for src, row, size in places:
                index = len(copies)
                at = where_ref[index] * rows + row
                copies.append(
                    pltpu.make_async_copy(
                        ref.at[src],
                        whole.at[pl.ds(pl.multiple_of(at, 16), size), pl.ds(col, ref.shape[-1])],
                        sems.at[index],
                    )
                )
        for copy in copies:
            copy.start()
        for copy in copies:
            copy.wait()
        out_own[...] = jnp.zeros_like(out_own)
        out_other[...] = jnp.zeros_like(out_other)

    merged = whole[pl.ds(pl.multiple_of(step * depth, depth), depth), :]
    out_other[...] += jnp.dot(other_ref[...], merged, preferred_element_type=F32)
    out_own[...] += jnp.dot(own_ref[...], merged, preferred_element_type=F32)


def project(acts, acts_other, chunks, slots, where, cols):
    tokens, width = acts.shape
    steps = 4
    out = jax.ShapeDtypeStruct((tokens, cols), F32)
    a_spec = pl.BlockSpec((tokens, width // steps), lambda i, *_: (0, i))
    o_spec = pl.BlockSpec((tokens, cols), lambda i, *_: (0, 0))
    return pl.pallas_call(
        functools.partial(out_kernel, slots=slots),
        grid_spec=pltpu.PrefetchScalarGridSpec(
            num_scalar_prefetch=1,
            grid=(steps,),
            in_specs=[a_spec, a_spec] + [pl.BlockSpec(memory_space=pl.ANY)] * len(chunks),
            out_specs=[o_spec, o_spec],
            scratch_shapes=[pltpu.VMEM((width, cols), BF16), pltpu.SemaphoreType.DMA((where.shape[0],))],
        ),
        out_shape=[out, out],
        compiler_params=pltpu.CompilerParams(vmem_limit_bytes=VMEM_LIMIT),
        cost_estimate=pl.CostEstimate(
            flops=4 * tokens * width * cols,
            bytes_accessed=4 * tokens * width + 2 * width * cols + 8 * tokens * cols,
            transcendentals=0,
        ),
        name="project",
    )(where, acts, acts_other, *chunks)


def on_device(acts, cotan, advantage, merge_ratio, weight, anchor, init):
    acts, cotan, levels, weight, anchor = acts[0], cotan[0], advantage[0], weight[0], anchor[0]
    tokens, width = acts.shape
    kv = cotan.shape[1]
    half = kv // 2
    blocks = XH * NZ
    own_rows = width // (blocks * NC)
    rows = own_rows * NC
    total_tokens = tokens * blocks * NC
    core, z, xh = lax.axis_index("c"), lax.axis_index("z"), lax.axis_index("xh")
    policy = lax.axis_index("xl") * NY + lax.axis_index("y")

    def my_half(a):
        return lax.dynamic_slice_in_dim(a, core * half, half, axis=-1)

    def other_half(a):
        return lax.dynamic_slice_in_dim(a, (1 - core) * half, half, axis=-1)

    def both_rows(mine, theirs):
        return jnp.where(core == 0, jnp.concatenate([mine, theirs], -2), jnp.concatenate([theirs, mine], -2))

    def both_cols(mine, theirs):
        return jnp.where(core == 0, jnp.concatenate([mine, theirs], -1), jnp.concatenate([theirs, mine], -1))

    given = jnp.stack([weight, init])
    given_got = swap(other_half(given), "c")
    acts_other = swap(after(acts, given_got), "c")
    given = both_rows(my_half(given), given_got)
    weight_half, init_half = given[0].astype(F32), given[1].astype(F32)
    init_up, init_down = shift(given[1], 1), shift(given[1], -1)

    *own, other_a, other_b = partial_grad(core, xh, levels, acts, cotan)
    early = (acts_other, init_up, init_down)
    got = [swap(after(other_a, *early), "c"), swap(after(other_b, *early), "c")]
    init_up2, init_down2 = shift(init_up, 1), shift(init_down, -1)
    init_near = jnp.stack([given[1], init_up, init_down, init_up2, init_down2])
    init_across = swap(init_near, "xh")
    streams = (0, 1)

    def pick(a, k, side, sides):
        cut = lax.dynamic_slice(a, (side, (z + k + NZ) % NZ, 0, 0), (sides, 1, rows, a.shape[-1]))
        return cut.reshape(sides, rows, -1).astype(F32)

    def term(s, k, side=0, sides=2):
        return pick(own[s], k, side, sides) + pick(got[s], k, side, sides)

    zero = ((0, 0), (0, 0))
    cut = rows // 2
    down, up, sums = [None, None], [None, None], [None, None]
    last = ()
    for k in (4, 3, 2, 1, 0):
        for s in streams:
            if k == 4:
                send_down, send_up = term(s, -4, 0, 1), term(s, 4, 1, 1)
                if s == 1:
                    send_down, send_up, *_ = tie(send_down, send_up, init_near, *last)
            else:
                down[s], up[s], *_ = tie(down[s], up[s], *last, *([init_across] if k == 1 else []))
                from_up, from_down = down[s].astype(F32), up[s].astype(F32)
                if k == 3:
                    from_up = jnp.pad(from_up, ((0, 1), *zero))
                    from_down = jnp.pad(from_down, ((1, 0), *zero))
                if k == 0:
                    sums[s] = term(s, 0) + from_up + from_down
                    send_down = send_up = sums[s][0].astype(BF16)
                else:
                    send_down, send_up = term(s, -k) + from_up, term(s, k) + from_down
            send_down, send_up = send_down.astype(BF16), send_up.astype(BF16)
            last = (send_down, send_up)
            if k == 0:
                down[s] = swap(send_down, "xh")
            else:
                down[s], up[s] = shift(send_down, -1), shift(send_up, 1)

    ratio = merge_ratio.astype(F32)
    shares = ratio / jnp.sum(ratio)
    share = shares[policy]
    bounds = ((0, COLS_A), (COLS_A, half))
    grads, mixes, norm = [None, None], [None, None], 0.0
    for s in streams:
        low, high = bounds[s]
        grads[s] = sums[s][1] + down[s].astype(F32)
        updated = weight_half[:, low:high] - step_size * grads[s] / math.sqrt(total_tokens)
        task = updated - init_half[:, low:high]
        norm = norm + jnp.sum(task * task)
        mixes[s] = (share * updated).astype(BF16)
    norms = jnp.where(lax.broadcasted_iota(jnp.int32, (8, 128), 0) == policy, norm, 0.0)
    last = ()
    for axis, bit in (("xl", 1), ("y", 1), ("y", 2)):
        arrived = [swap(mixes[0], axis, bit), swap(mixes[1], axis, bit)]
        norms_got = swap(after(norms, mixes[1]), axis, bit)
        for s in streams:
            if s == 1:
                arrived[s], norms_got, *_ = tie(arrived[s], norms_got, mixes[0])
                norms = norms + norms_got
            mixes[s] = mixes[s].astype(F32) + arrived[s].astype(F32)
            if (axis, bit) != ("y", 2):
                mixes[s] = mixes[s].astype(BF16)
    mixed_sq = 0.0
    for s in streams:
        low, high = bounds[s]
        mixed = mixes[s] - init_half[:, low:high]
        mixed_sq = mixed_sq + jnp.sum(mixed * mixed)
    scalars = jnp.where(lax.broadcasted_iota(jnp.int32, (8, 128), 1) == 0, norms, mixed_sq)

    def add_over(scalars, axis, bit, *others):
        scalars = after(scalars, *others)
        return scalars + swap(scalars, axis, bit)

    blocks_sent = [m.astype(BF16) for m in mixes]
    across = [swap(a, "xh") for a in blocks_sent]
    scalars = add_over(scalars, "c", 1, *blocks_sent)
    pairs = [jnp.stack([a, b]) for a, b in zip(blocks_sent, across)]
    up, down = [shift(pairs[0], 1), None], [shift(pairs[0], -1), None]
    pairs[1] = after(pairs[1], pairs[0])
    up[1], down[1] = shift(pairs[1], 1), shift(pairs[1], -1)
    scalars = add_over(scalars, "xh", 1, pairs[1])
    scalars = add_over(scalars, "z", 1)

    def merge(k, mix, s):
        low, high = bounds[s]
        at = {0: 0, -1: 1, 1: 2, -2: 3, 2: 4}[k]
        base = jnp.stack([init_near[at, :, low:high], init_across[at, :, low:high]]).astype(F32)
        return (base + (mix.astype(F32) - base) * factor).astype(BF16)

    chunks = [[], []]
    last = ()
    for k in (2, 3, 4):
        for s in streams:
            up[s], down[s], *_ = tie(up[s], down[s], *last)
            if k == 2 and s == 0:
                scalars = add_over(scalars, "z", 2)
            if k == 2 and s == 1:
                scalars = add_over(scalars, "z", 4, up[1])
                target = jnp.sum(shares * jnp.sqrt(scalars[:, 0]))
                factor = target / jnp.sqrt(scalars[0, 1])
            if k == 3:
                up[s], down[s] = merge(-2, up[s], s), merge(2, down[s], s)
            chunks[s] += [(up[s], 1 - k), (down[s], k - 1)]
            if k == 4:
                up[s], down[s] = up[s][:, :cut], down[s][:, cut:]
            last = (up[s], down[s])
            up[s], down[s] = shift(up[s], 1), shift(down[s], -1)

    def place(x, k):
        return (x * NZ + (z + k + NZ) % NZ).astype(jnp.int32)

    arrays, slots, where, merged = [], [], [], []
    for s in streams:
        (up1, _), (down1, _), *rest = chunks[s]
        mine = merge(0, pairs[s], s)
        merged.append(mine[0])
        for array, k in [(mine, 0), (merge(-1, up1, s), -1), (merge(1, down1, s), 1)] + rest:
            arrays.append(array)
            slots.append((bounds[s][0], [(0, 0, rows), (1, 0, rows)]))
            where += [place(xh, k), place(1 - xh, k)]
        for array, row, size in ((up[s], 0, cut), (down[s], cut, rows - cut)):
            arrays.append(array)
            slots.append((bounds[s][0], [(0, row, size), (1, row, size)]))
            where += [place(xh, 4), place(1 - xh, 4)]
    mine, away = project(acts, acts_other, arrays, slots, jnp.stack(where), half)
    result = both_cols(mine, swap(away, "c"))
    merged = jnp.concatenate(merged, axis=1)
    grad = jnp.concatenate(grads, axis=1)

    def to_rows(a):
        mine = lax.dynamic_slice_in_dim(a, core * own_rows, own_rows, axis=0)
        theirs = lax.dynamic_slice_in_dim(a, (1 - core) * own_rows, own_rows, axis=0)
        return both_cols(mine, swap(theirs, "c"))

    grad_rows = to_rows(grad.astype(BF16)).astype(F32)
    anchor_new = ema_decay * anchor + (1.0 - ema_decay) * (
        weight.astype(F32) - step_size * grad_rows / math.sqrt(total_tokens)
    )
    return anchor_new[None], to_rows(merged), result[None]


def solution(mesh):
    mesh = Mesh(mesh.devices.reshape(XL, NY, XH, NZ, NC), ("xl", "y", "xh", "z", "c"))
    policy, zero = ("xl", "y"), ("xh", "z", "c")
    placed = (
        P(policy, zero, None),
        P(policy, zero, None),
        P(policy, zero),
        P(),
        P(policy, zero, None),
        P(policy, zero, None),
        P(zero, None),
    )
    return jax.shard_map(
        on_device,
        mesh=mesh,
        in_specs=placed,
        out_specs=(P(policy, zero, None), P(zero, None), P(policy, zero, None)),
        check_vma=False,
    )
```

```python
import functools
import math

import jax
import jax.numpy as jnp
from jax import lax
from jax.experimental import pallas as pl
from jax.experimental.pallas import tpu as pltpu
from jax.sharding import Mesh, PartitionSpec as P

SEQ = 128
step_size = 0.02
ema_decay = 0.9

XL, NY, XH, NZ, NC = 2, 4, 2, 8, 2
F32, BF16 = jnp.float32, jnp.bfloat16

COLS_A = 256
VMEM_LIMIT = 56 * 1024 * 1024


def swap(a, axis, bit=1):
    size = {"xl": XL, "y": NY, "xh": XH, "z": NZ, "c": NC}[axis]
    return lax.ppermute(a, axis, [(i, i ^ bit) for i in range(size)])


def shift(a, by):
    return lax.ppermute(a, "z", [(i, (i + by) % NZ) for i in range(NZ)])


def after(a, *others):
    return lax.optimization_barrier((a, others))[0]


def tie(*arrays):
    return lax.optimization_barrier(arrays)


def grad_kernel(where_ref, level_ref, acts_ref, cotan_ref, *refs):
    outs, scaled_ref = refs[:4], refs[4]
    half = scaled_ref.shape[1] // 2

    @pl.when(pl.program_id(0) == 0)
    def _():
        first = where_ref[0] == 0
        for seq in range(level_ref.shape[0]):
            rows = pl.ds(seq * SEQ, SEQ)
            level = level_ref[seq].astype(F32) * 0.25
            low, high = cotan_ref[rows, :half], cotan_ref[rows, half:]
            scaled_ref[rows, :half] = (jnp.where(first, low, high).astype(F32) * level).astype(BF16)
            scaled_ref[rows, half:] = (jnp.where(first, high, low).astype(F32) * level).astype(BF16)

    product = lax.dot_general(
        acts_ref[...], scaled_ref[...], (((0,), (0,)), ((), ())), preferred_element_type=F32
    ).astype(BF16)
    at = 0
    for out in outs:
        cols = out.shape[-1]
        out[...] = product[:, at : at + cols].reshape(out.shape)
        at += cols


def partial_grad(core, side, levels, acts, cotan):
    tokens, width = acts.shape
    kv = cotan.shape[1]
    rows = width // (XH * NZ)
    steps = 2
    outs, specs = [], []
    for cols in (COLS_A, kv // 2 - COLS_A) * 2:
        outs.append(jax.ShapeDtypeStruct((XH, NZ, rows, cols), BF16))
        specs.append(pl.BlockSpec((1, NZ // steps, rows, cols), lambda i, *_: (i // steps, i % steps, 0, 0)))

    def block(i, at, _):
        return 0, jnp.where(i < steps, 1 - at[1], at[1]) * steps + i % steps

    return pl.pallas_call(
        grad_kernel,
        grid_spec=pltpu.PrefetchScalarGridSpec(
            num_scalar_prefetch=2,
            grid=(XH * steps,),
            in_specs=[
                pl.BlockSpec((tokens, width // (XH * steps)), block),
                pl.BlockSpec((tokens, kv), lambda i, *_: (0, 0)),
            ],
            out_specs=specs,
            scratch_shapes=[pltpu.VMEM((tokens, kv), BF16)],
        ),
        out_shape=outs,
        compiler_params=pltpu.CompilerParams(vmem_limit_bytes=VMEM_LIMIT),
        cost_estimate=pl.CostEstimate(
            flops=2 * tokens * width * kv,
            bytes_accessed=2 * (tokens * width + tokens * kv + width * kv),
            transcendentals=0,
        ),
        name="partial_grad",
    )(jnp.stack([core, side]).astype(jnp.int32), levels, acts, cotan)


def out_kernel(where_ref, own_ref, other_ref, *refs, slots):
    chunks, (out_own, out_other, whole, sems) = refs[: len(slots)], refs[len(slots) :]
    rows = whole.shape[0] // (XH * NZ)
    step = pl.program_id(0)
    depth = own_ref.shape[1]

    @pl.when(step == 0)
    def _():
        copies = []
        for ref, (col, places) in zip(chunks, slots):
            for src, row, size in places:
                index = len(copies)
                at = where_ref[index] * rows + row
                copies.append(
                    pltpu.make_async_copy(
                        ref.at[src],
                        whole.at[pl.ds(pl.multiple_of(at, 16), size), pl.ds(col, ref.shape[-1])],
                        sems.at[index],
                    )
                )
        for copy in copies:
            copy.start()
        for copy in copies:
            copy.wait()
        out_own[...] = jnp.zeros_like(out_own)
        out_other[...] = jnp.zeros_like(out_other)

    merged = whole[pl.ds(pl.multiple_of(step * depth, depth), depth), :]
    out_other[...] += jnp.dot(other_ref[...], merged, preferred_element_type=F32)
    out_own[...] += jnp.dot(own_ref[...], merged, preferred_element_type=F32)


def project(acts, acts_other, chunks, slots, where, cols):
    tokens, width = acts.shape
    steps = 4
    out = jax.ShapeDtypeStruct((tokens, cols), F32)
    a_spec = pl.BlockSpec((tokens, width // steps), lambda i, *_: (0, i))
    o_spec = pl.BlockSpec((tokens, cols), lambda i, *_: (0, 0))
    return pl.pallas_call(
        functools.partial(out_kernel, slots=slots),
        grid_spec=pltpu.PrefetchScalarGridSpec(
            num_scalar_prefetch=1,
            grid=(steps,),
            in_specs=[a_spec, a_spec] + [pl.BlockSpec(memory_space=pl.ANY)] * len(chunks),
            out_specs=[o_spec, o_spec],
            scratch_shapes=[pltpu.VMEM((width, cols), BF16), pltpu.SemaphoreType.DMA((where.shape[0],))],
        ),
        out_shape=[out, out],
        compiler_params=pltpu.CompilerParams(vmem_limit_bytes=VMEM_LIMIT),
        cost_estimate=pl.CostEstimate(
            flops=4 * tokens * width * cols,
            bytes_accessed=4 * tokens * width + 2 * width * cols + 8 * tokens * cols,
            transcendentals=0,
        ),
        name="project",
    )(where, acts, acts_other, *chunks)


def on_device(acts, cotan, advantage, merge_ratio, weight, anchor, init):
    acts, cotan, levels, weight, anchor = acts[0], cotan[0], advantage[0], weight[0], anchor[0]
    tokens, width = acts.shape
    kv = cotan.shape[1]
    half = kv // 2
    blocks = XH * NZ
    own_rows = width // (blocks * NC)
    rows = own_rows * NC
    total_tokens = tokens * blocks * NC
    core, z, xh = lax.axis_index("c"), lax.axis_index("z"), lax.axis_index("xh")
    policy = lax.axis_index("xl") * NY + lax.axis_index("y")

    def my_half(a):
        return lax.dynamic_slice_in_dim(a, core * half, half, axis=-1)

    def other_half(a):
        return lax.dynamic_slice_in_dim(a, (1 - core) * half, half, axis=-1)

    def both_rows(mine, theirs):
        return jnp.where(core == 0, jnp.concatenate([mine, theirs], -2), jnp.concatenate([theirs, mine], -2))

    def both_cols(mine, theirs):
        return jnp.where(core == 0, jnp.concatenate([mine, theirs], -1), jnp.concatenate([theirs, mine], -1))

    given = jnp.stack([weight, init])
    given_got = swap(other_half(given), "c")
    acts_other = swap(after(acts, given_got), "c")
    given = both_rows(my_half(given), given_got)
    weight_half, init_half = given[0].astype(F32), given[1].astype(F32)
    init_up, init_down = shift(given[1], 1), shift(given[1], -1)

    *own, other_a, other_b = partial_grad(core, xh, levels, acts, cotan)
    early = (acts_other, init_up, init_down)
    got = [swap(after(other_a, *early), "c"), swap(after(other_b, *early), "c")]
    init_near = jnp.stack([given[1], init_up, init_down])
    init_across = swap(init_near, "xh")
    streams = (0, 1)

    def pick(a, k, side, sides):
        cut = lax.dynamic_slice(a, (side, (z + k + NZ) % NZ, 0, 0), (sides, 1, rows, a.shape[-1]))
        return cut.reshape(sides, rows, -1).astype(F32)

    def term(s, k, side=0, sides=2):
        return pick(own[s], k, side, sides) + pick(got[s], k, side, sides)

    zero = ((0, 0), (0, 0))
    cut = rows // 2
    down, up, sums = [None, None], [None, None], [None, None]
    last = ()
    ahead = {(3, 1): (init_across,)}
    for k in (4, 3, 2, 1, 0):
        for s in streams:
            if k == 4:
                send_down, send_up = term(s, -4, 0, 1), term(s, 4, 1, 1)
                if s == 1:
                    send_down, send_up, *_ = tie(send_down, send_up, *last)
            else:
                down[s], up[s], *_ = tie(down[s], up[s], *last, *ahead.get((k, s), ()))
                from_up, from_down = down[s].astype(F32), up[s].astype(F32)
                if k == 3:
                    from_up = jnp.pad(from_up, ((0, 1), *zero))
                    from_down = jnp.pad(from_down, ((1, 0), *zero))
                if k == 0:
                    sums[s] = term(s, 0) + from_up + from_down
                    send_down = send_up = sums[s][0].astype(BF16)
                else:
                    send_down, send_up = term(s, -k) + from_up, term(s, k) + from_down
            send_down, send_up = send_down.astype(BF16), send_up.astype(BF16)
            last = (send_down, send_up)
            if (k, s) == (3, 0):
                init_far = jnp.stack([shift(after(init_up, *last), 1), shift(after(init_down, *last), -1)])
                init_far_across = swap(init_far, "xh")
                ahead[1, 0] = (init_far,)
                ahead[0, 0] = (init_far_across,)
            if k == 0:
                down[s] = swap(send_down, "xh")
            else:
                down[s], up[s] = shift(send_down, -1), shift(send_up, 1)

    ratio = merge_ratio.astype(F32)
    shares = ratio / jnp.sum(ratio)
    share = shares[policy]
    bounds = ((0, COLS_A), (COLS_A, half))
    grads, mixes, norm = [None, None], [None, None], 0.0
    for s in streams:
        low, high = bounds[s]
        grads[s] = sums[s][1] + down[s].astype(F32)
        updated = weight_half[:, low:high] - step_size * grads[s] / math.sqrt(total_tokens)
        task = updated - init_half[:, low:high]
        norm = norm + jnp.sum(task * task)
        mixes[s] = (share * updated).astype(BF16)
    norms = jnp.where(lax.broadcasted_iota(jnp.int32, (8, 128), 0) == policy, norm, 0.0)
    last = ()
    for axis, bit in (("xl", 1), ("y", 1), ("y", 2)):
        arrived = [swap(mixes[0], axis, bit), swap(mixes[1], axis, bit)]
        norms_got = swap(after(norms, mixes[1]), axis, bit)
        for s in streams:
            if s == 1:
                arrived[s], norms_got, *_ = tie(arrived[s], norms_got, mixes[0])
                norms = norms + norms_got
            mixes[s] = mixes[s].astype(F32) + arrived[s].astype(F32)
            if (axis, bit) != ("y", 2):
                mixes[s] = mixes[s].astype(BF16)
    mixed_sq = 0.0
    for s in streams:
        low, high = bounds[s]
        mixed = mixes[s] - init_half[:, low:high]
        mixed_sq = mixed_sq + jnp.sum(mixed * mixed)
    scalars = jnp.where(lax.broadcasted_iota(jnp.int32, (8, 128), 1) == 0, norms, mixed_sq)

    def add_over(scalars, axis, bit, *others):
        scalars = after(scalars, *others)
        return scalars + swap(scalars, axis, bit)

    blocks_sent = [m.astype(BF16) for m in mixes]
    across = [swap(a, "xh") for a in blocks_sent]
    scalars = add_over(scalars, "z", 1, *blocks_sent)
    scalars = add_over(scalars, "z", 2)
    pairs = [jnp.stack([a, b]) for a, b in zip(blocks_sent, across)]
    up, down = [shift(pairs[0], 1), None], [shift(pairs[0], -1), None]
    pairs[1] = after(pairs[1], pairs[0])
    up[1], down[1] = shift(pairs[1], 1), shift(pairs[1], -1)
    far_scalars = swap(after(scalars, pairs[1]), "z", 4)

    def merge(k, mix, s):
        low, high = bounds[s]
        here, there = (init_far, init_far_across) if abs(k) == 2 else (init_near, init_across)
        at = {0: 0, -1: 1, 1: 2, -2: 0, 2: 1}[k]
        base = jnp.stack([here[at, :, low:high], there[at, :, low:high]]).astype(F32)
        return (base + (mix.astype(F32) - base) * factor).astype(BF16)

    def to_rows(a):
        mine = lax.dynamic_slice_in_dim(a, core * own_rows, own_rows, axis=0)
        theirs = lax.dynamic_slice_in_dim(a, (1 - core) * own_rows, own_rows, axis=0)
        return both_cols(mine, swap(theirs, "c"))

    grad_rows = to_rows(jnp.concatenate(grads, axis=1).astype(BF16)).astype(F32)
    anchor_new = ema_decay * anchor + (1.0 - ema_decay) * (
        weight.astype(F32) - step_size * grad_rows / math.sqrt(total_tokens)
    )

    chunks = [[], []]
    last = ()
    for k in (2, 3, 4):
        for s in streams:
            up[s], down[s], *_ = tie(up[s], down[s], *last)
            if k == 2 and s == 0:
                up[0], down[0], far_scalars = tie(up[0], down[0], far_scalars)
                scalars = add_over(scalars + far_scalars, "c", 1)
            if k == 2 and s == 1:
                scalars = add_over(scalars, "xh", 1, up[1])
                target = jnp.sum(shares * jnp.sqrt(scalars[:, 0]))
                factor = target / jnp.sqrt(scalars[0, 1])
            if k == 3 and s == 0:
                up[0], anchor_new = tie(up[0], anchor_new)
            if k == 3:
                up[s], down[s] = merge(-2, up[s], s), merge(2, down[s], s)
            chunks[s] += [(up[s], 1 - k), (down[s], k - 1)]
            if k == 4:
                up[s], down[s] = up[s][:, :cut], down[s][:, cut:]
            last = (up[s], down[s])
            up[s], down[s] = shift(up[s], 1), shift(down[s], -1)

    def place(x, k):
        return (x * NZ + (z + k + NZ) % NZ).astype(jnp.int32)

    arrays, slots, where, merged = [], [], [], []
    for s in streams:
        (up1, _), (down1, _), *rest = chunks[s]
        mine = merge(0, pairs[s], s)
        merged.append(mine[0])
        for array, k in [(mine, 0), (merge(-1, up1, s), -1), (merge(1, down1, s), 1)] + rest:
            arrays.append(array)
            slots.append((bounds[s][0], [(0, 0, rows), (1, 0, rows)]))
            where += [place(xh, k), place(1 - xh, k)]
        for array, row, size in ((up[s], 0, cut), (down[s], cut, rows - cut)):
            arrays.append(array)
            slots.append((bounds[s][0], [(0, row, size), (1, row, size)]))
            where += [place(xh, 4), place(1 - xh, 4)]
    merged_rows = to_rows(jnp.concatenate(merged, axis=1))
    mine, away = project(acts, acts_other, arrays, slots, after(jnp.stack(where), merged_rows), half)
    result = both_cols(mine, swap(away, "c"))
    return anchor_new[None], merged_rows, result[None]


def solution(mesh):
    mesh = Mesh(mesh.devices.reshape(XL, NY, XH, NZ, NC), ("xl", "y", "xh", "z", "c"))
    policy, zero = ("xl", "y"), ("xh", "z", "c")
    placed = (
        P(policy, zero, None),
        P(policy, zero, None),
        P(policy, zero),
        P(),
        P(policy, zero, None),
        P(policy, zero, None),
        P(zero, None),
    )
    return jax.shard_map(
        on_device,
        mesh=mesh,
        in_specs=placed,
        out_specs=(P(policy, zero, None), P(zero, None), P(policy, zero, None)),
        check_vma=False,
    )
```

```python
import functools
import math

import jax
import jax.numpy as jnp
from jax import lax
from jax.experimental import pallas as pl
from jax.experimental.pallas import tpu as pltpu
from jax.sharding import Mesh, PartitionSpec as P

SEQ = 128
step_size = 0.02
ema_decay = 0.9

XL, NY, XH, NZ, NC = 2, 4, 2, 8, 2
F32, BF16 = jnp.float32, jnp.bfloat16

COLS_A = 256
VMEM_LIMIT = 56 * 1024 * 1024


def swap(a, axis, bit=1):
    size = {"xl": XL, "y": NY, "xh": XH, "z": NZ, "c": NC}[axis]
    return lax.ppermute(a, axis, [(i, i ^ bit) for i in range(size)])


def shift(a, by):
    return lax.ppermute(a, "z", [(i, (i + by) % NZ) for i in range(NZ)])


def after(a, *others):
    return lax.optimization_barrier((a, others))[0]


def tie(*arrays):
    return lax.optimization_barrier(arrays)


def grad_kernel(where_ref, level_ref, acts_ref, cotan_ref, *refs):
    outs, scaled_ref = refs[:4], refs[4]
    half = scaled_ref.shape[1] // 2

    @pl.when(pl.program_id(0) == 0)
    def _():
        first = where_ref[0] == 0
        for seq in range(level_ref.shape[0]):
            rows = pl.ds(seq * SEQ, SEQ)
            level = level_ref[seq].astype(F32) * 0.25
            low, high = cotan_ref[rows, :half], cotan_ref[rows, half:]
            scaled_ref[rows, :half] = (jnp.where(first, low, high).astype(F32) * level).astype(BF16)
            scaled_ref[rows, half:] = (jnp.where(first, high, low).astype(F32) * level).astype(BF16)

    product = lax.dot_general(
        acts_ref[...], scaled_ref[...], (((0,), (0,)), ((), ())), preferred_element_type=F32
    ).astype(BF16)
    at = 0
    for out in outs:
        cols = out.shape[-1]
        out[...] = product[:, at : at + cols].reshape(out.shape)
        at += cols


def partial_grad(core, side, levels, acts, cotan):
    tokens, width = acts.shape
    kv = cotan.shape[1]
    rows = width // (XH * NZ)
    steps = 2
    outs, specs = [], []
    for cols in (COLS_A, kv // 2 - COLS_A) * 2:
        outs.append(jax.ShapeDtypeStruct((XH, NZ, rows, cols), BF16))
        specs.append(pl.BlockSpec((1, NZ // steps, rows, cols), lambda i, *_: (i // steps, i % steps, 0, 0)))

    def block(i, at, _):
        return 0, jnp.where(i < steps, 1 - at[1], at[1]) * steps + i % steps

    return pl.pallas_call(
        grad_kernel,
        grid_spec=pltpu.PrefetchScalarGridSpec(
            num_scalar_prefetch=2,
            grid=(XH * steps,),
            in_specs=[
                pl.BlockSpec((tokens, width // (XH * steps)), block),
                pl.BlockSpec((tokens, kv), lambda i, *_: (0, 0)),
            ],
            out_specs=specs,
            scratch_shapes=[pltpu.VMEM((tokens, kv), BF16)],
        ),
        out_shape=outs,
        compiler_params=pltpu.CompilerParams(vmem_limit_bytes=VMEM_LIMIT),
        cost_estimate=pl.CostEstimate(
            flops=2 * tokens * width * kv,
            bytes_accessed=2 * (tokens * width + tokens * kv + width * kv),
            transcendentals=0,
        ),
        name="partial_grad",
    )(jnp.stack([core, side]).astype(jnp.int32), levels, acts, cotan)


def out_kernel(where_ref, acts_ref, *refs, slots):
    chunks, (out, whole, sems) = refs[: len(slots)], refs[len(slots) :]
    rows = whole.shape[0] // (XH * NZ)
    step = pl.program_id(0)
    depth = acts_ref.shape[1]

    @pl.when(step == 0)
    def _():
        copies = []
        for ref, (col, places) in zip(chunks, slots):
            for src, row, size in places:
                index = len(copies)
                at = where_ref[index] * rows + row
                copies.append(
                    pltpu.make_async_copy(
                        ref.at[src],
                        whole.at[pl.ds(pl.multiple_of(at, 16), size), pl.ds(col, ref.shape[-1])],
                        sems.at[index],
                    )
                )
        for copy in copies:
            copy.start()
        for copy in copies:
            copy.wait()
        out[...] = jnp.zeros_like(out)

    merged = whole[pl.ds(pl.multiple_of(step * depth, depth), depth), :]
    out[...] += jnp.dot(acts_ref[...], merged, preferred_element_type=F32)


def project(acts, chunks, slots, where, cols, total):
    tokens, width = acts.shape
    steps = 4
    count = where.shape[0] - 1
    return pl.pallas_call(
        functools.partial(out_kernel, slots=slots),
        grid_spec=pltpu.PrefetchScalarGridSpec(
            num_scalar_prefetch=1,
            grid=(steps,),
            in_specs=[pl.BlockSpec((tokens, width // steps), lambda i, *_: (0, i))]
            + [pl.BlockSpec(memory_space=pl.ANY)] * len(chunks),
            out_specs=pl.BlockSpec((tokens, cols), lambda i, at: (0, at[count])),
            scratch_shapes=[pltpu.VMEM((width, cols), BF16), pltpu.SemaphoreType.DMA((count,))],
        ),
        out_shape=jax.ShapeDtypeStruct((tokens, total), F32),
        compiler_params=pltpu.CompilerParams(vmem_limit_bytes=VMEM_LIMIT),
        cost_estimate=pl.CostEstimate(
            flops=2 * tokens * width * cols,
            bytes_accessed=2 * tokens * width + 2 * width * cols + 4 * tokens * cols,
            transcendentals=0,
        ),
        name="project",
    )(where, acts, *chunks)


def place_kernel(at_ref, columns_ref, whole_ref, out_ref):
    out_ref[...] = columns_ref[...]


def place_columns(at, columns, whole):
    tokens, cols = columns.shape
    steps = 4
    return pl.pallas_call(
        place_kernel,
        grid_spec=pltpu.PrefetchScalarGridSpec(
            num_scalar_prefetch=1,
            grid=(steps,),
            in_specs=[
                pl.BlockSpec((tokens // steps, cols), lambda i, _: (i, 0)),
                pl.BlockSpec(memory_space=pl.ANY),
            ],
            out_specs=pl.BlockSpec((tokens // steps, cols), lambda i, at: (i, at[0])),
        ),
        out_shape=jax.ShapeDtypeStruct(whole.shape, F32),
        input_output_aliases={2: 0},
        compiler_params=pltpu.CompilerParams(vmem_limit_bytes=VMEM_LIMIT),
        cost_estimate=pl.CostEstimate(flops=0, bytes_accessed=8 * tokens * cols, transcendentals=0),
        name="place_columns",
    )(at, columns, whole)


def on_device(acts, cotan, advantage, merge_ratio, weight, anchor, init):
    acts, cotan, levels, weight, anchor = acts[0], cotan[0], advantage[0], weight[0], anchor[0]
    tokens, width = acts.shape
    kv = cotan.shape[1]
    half = kv // 2
    blocks = XH * NZ
    own_rows = width // (blocks * NC)
    rows = own_rows * NC
    total_tokens = tokens * blocks * NC
    core, z, xh = lax.axis_index("c"), lax.axis_index("z"), lax.axis_index("xh")
    policy = lax.axis_index("xl") * NY + lax.axis_index("y")

    def my_half(a):
        return lax.dynamic_slice_in_dim(a, core * half, half, axis=-1)

    def other_half(a):
        return lax.dynamic_slice_in_dim(a, (1 - core) * half, half, axis=-1)

    def both_rows(mine, theirs):
        return jnp.where(core == 0, jnp.concatenate([mine, theirs], -2), jnp.concatenate([theirs, mine], -2))

    def both_cols(mine, theirs):
        return jnp.where(core == 0, jnp.concatenate([mine, theirs], -1), jnp.concatenate([theirs, mine], -1))

    given = jnp.stack([weight, init])
    given_got = swap(other_half(given), "c")
    acts_other = swap(after(acts, given_got), "c")
    given = both_rows(my_half(given), given_got)
    weight_half, init_half = given[0].astype(F32), given[1].astype(F32)
    init_up, init_down = shift(given[1], 1), shift(given[1], -1)

    *own, other_a, other_b = partial_grad(core, xh, levels, acts, cotan)
    early = (acts_other, init_up, init_down)
    got = [swap(after(other_a, *early), "c"), swap(after(other_b, *early), "c")]
    init_near = jnp.stack([given[1], init_up, init_down])
    init_across = swap(init_near, "xh")
    streams = (0, 1)

    def pick(a, k, side, sides):
        cut = lax.dynamic_slice(a, (side, (z + k + NZ) % NZ, 0, 0), (sides, 1, rows, a.shape[-1]))
        return cut.reshape(sides, rows, -1).astype(F32)

    def term(s, k, side=0, sides=2):
        return pick(own[s], k, side, sides) + pick(got[s], k, side, sides)

    zero = ((0, 0), (0, 0))
    cut = rows // 2
    down, up, sums = [None, None], [None, None], [None, None]
    last = ()
    ahead = {(3, 1): (init_across,)}
    for k in (4, 3, 2, 1, 0):
        for s in streams:
            if k == 4:
                send_down, send_up = term(s, -4, 0, 1), term(s, 4, 1, 1)
                if s == 1:
                    send_down, send_up, *_ = tie(send_down, send_up, *last)
            else:
                down[s], up[s], *_ = tie(down[s], up[s], *last, *ahead.get((k, s), ()))
                from_up, from_down = down[s].astype(F32), up[s].astype(F32)
                if k == 3:
                    from_up = jnp.pad(from_up, ((0, 1), *zero))
                    from_down = jnp.pad(from_down, ((1, 0), *zero))
                if k == 0:
                    sums[s] = term(s, 0) + from_up + from_down
                    send_down = send_up = sums[s][0].astype(BF16)
                else:
                    send_down, send_up = term(s, -k) + from_up, term(s, k) + from_down
            send_down, send_up = send_down.astype(BF16), send_up.astype(BF16)
            last = (send_down, send_up)
            if (k, s) == (3, 0):
                init_far = jnp.stack([shift(after(init_up, *last), 1), shift(after(init_down, *last), -1)])
                init_far_across = swap(init_far, "xh")
                ahead[1, 0] = (init_far,)
                ahead[0, 0] = (init_far_across,)
            if k == 0:
                down[s] = swap(send_down, "xh")
            else:
                down[s], up[s] = shift(send_down, -1), shift(send_up, 1)

    ratio = merge_ratio.astype(F32)
    shares = ratio / jnp.sum(ratio)
    share = shares[policy]
    bounds = ((0, COLS_A), (COLS_A, half))
    grads, mixes, norm = [None, None], [None, None], 0.0
    for s in streams:
        low, high = bounds[s]
        grads[s] = sums[s][1] + down[s].astype(F32)
        updated = weight_half[:, low:high] - step_size * grads[s] / math.sqrt(total_tokens)
        task = updated - init_half[:, low:high]
        norm = norm + jnp.sum(task * task)
        mixes[s] = (share * updated).astype(BF16)
    norms = jnp.where(lax.broadcasted_iota(jnp.int32, (8, 128), 0) == policy, norm, 0.0)
    last = ()
    for axis, bit in (("xl", 1), ("y", 1), ("y", 2)):
        arrived = [swap(mixes[0], axis, bit), swap(mixes[1], axis, bit)]
        norms_got = swap(after(norms, mixes[1]), axis, bit)
        for s in streams:
            if s == 1:
                arrived[s], norms_got, *_ = tie(arrived[s], norms_got, mixes[0])
                norms = norms + norms_got
            mixes[s] = mixes[s].astype(F32) + arrived[s].astype(F32)
            if (axis, bit) != ("y", 2):
                mixes[s] = mixes[s].astype(BF16)
    mixed_sq = 0.0
    for s in streams:
        low, high = bounds[s]
        mixed = mixes[s] - init_half[:, low:high]
        mixed_sq = mixed_sq + jnp.sum(mixed * mixed)
    scalars = jnp.where(lax.broadcasted_iota(jnp.int32, (8, 128), 1) == 0, norms, mixed_sq)

    def add_over(scalars, axis, bit, *others):
        scalars = after(scalars, *others)
        return scalars + swap(scalars, axis, bit)

    blocks_sent = [m.astype(BF16) for m in mixes]
    across = [swap(a, "xh") for a in blocks_sent]
    scalars = add_over(scalars, "z", 1, *blocks_sent)
    scalars = add_over(scalars, "z", 2)
    pairs = [jnp.stack([a, b]) for a, b in zip(blocks_sent, across)]
    up, down = [shift(pairs[0], 1), None], [shift(pairs[0], -1), None]
    pairs[1] = after(pairs[1], pairs[0])
    up[1], down[1] = shift(pairs[1], 1), shift(pairs[1], -1)
    far_scalars = swap(after(scalars, pairs[1]), "z", 4)

    def merge(k, mix, s):
        low, high = bounds[s]
        here, there = (init_far, init_far_across) if abs(k) == 2 else (init_near, init_across)
        at = {0: 0, -1: 1, 1: 2, -2: 0, 2: 1}[k]
        base = jnp.stack([here[at, :, low:high], there[at, :, low:high]]).astype(F32)
        return (base + (mix.astype(F32) - base) * factor).astype(BF16)

    def to_rows(a):
        mine = lax.dynamic_slice_in_dim(a, core * own_rows, own_rows, axis=0)
        theirs = lax.dynamic_slice_in_dim(a, (1 - core) * own_rows, own_rows, axis=0)
        return both_cols(mine, swap(theirs, "c"))

    grad_rows = to_rows(jnp.concatenate(grads, axis=1).astype(BF16)).astype(F32)
    anchor_new = ema_decay * anchor + (1.0 - ema_decay) * (
        weight.astype(F32) - step_size * grad_rows / math.sqrt(total_tokens)
    )

    chunks = [[], []]
    last = ()
    for k in (2, 3, 4):
        for s in streams:
            up[s], down[s], *_ = tie(up[s], down[s], *last)
            if k == 2 and s == 0:
                up[0], down[0], far_scalars = tie(up[0], down[0], far_scalars)
                scalars = add_over(scalars + far_scalars, "c", 1)
            if k == 2 and s == 1:
                scalars = add_over(scalars, "xh", 1, up[1])
                target = jnp.sum(shares * jnp.sqrt(scalars[:, 0]))
                factor = target / jnp.sqrt(scalars[0, 1])
            if k == 3 and s == 0:
                up[0], anchor_new = tie(up[0], anchor_new)
            if k == 3:
                up[s], down[s] = merge(-2, up[s], s), merge(2, down[s], s)
            chunks[s] += [(up[s], 1 - k), (down[s], k - 1)]
            if k == 4:
                up[s], down[s] = up[s][:, :cut], down[s][:, cut:]
            last = (up[s], down[s])
            up[s], down[s] = shift(up[s], 1), shift(down[s], -1)

    def place(x, k):
        return (x * NZ + (z + k + NZ) % NZ).astype(jnp.int32)

    arrays, slots, where, merged = [], [], [], []
    for s in streams:
        (up1, _), (down1, _), *rest = chunks[s]
        mine = merge(0, pairs[s], s)
        merged.append(mine[0])
        for array, k in [(mine, 0), (merge(-1, up1, s), -1), (merge(1, down1, s), 1)] + rest:
            arrays.append(array)
            slots.append((bounds[s][0], [(0, 0, rows), (1, 0, rows)]))
            where += [place(xh, k), place(1 - xh, k)]
        for array, row, size in ((up[s], 0, cut), (down[s], cut, rows - cut)):
            arrays.append(array)
            slots.append((bounds[s][0], [(0, row, size), (1, row, size)]))
            where += [place(xh, 4), place(1 - xh, 4)]
    merged_rows = to_rows(jnp.concatenate(merged, axis=1))
    where = after(jnp.stack(where), merged_rows)
    here = core.astype(jnp.int32).reshape(1)
    away = project(acts_other, arrays, slots, jnp.concatenate([where, jnp.zeros_like(here)]), half, half)
    home = swap(away, "c")
    result = project(after(acts, away), arrays, slots, jnp.concatenate([where, here]), half, kv)
    result = place_columns(1 - here, home, result)

    return anchor_new[None], merged_rows, result[None]


def solution(mesh):
    mesh = Mesh(mesh.devices.reshape(XL, NY, XH, NZ, NC), ("xl", "y", "xh", "z", "c"))
    policy, zero = ("xl", "y"), ("xh", "z", "c")
    placed = (
        P(policy, zero, None),
        P(policy, zero, None),
        P(policy, zero),
        P(),
        P(policy, zero, None),
        P(policy, zero, None),
        P(zero, None),
    )
    return jax.shard_map(
        on_device,
        mesh=mesh,
        in_specs=placed,
        out_specs=(P(policy, zero, None), P(zero, None), P(policy, zero, None)),
        check_vma=False,
    )
```

```python
import functools
import math

import jax
import jax.numpy as jnp
from jax import lax
from jax.experimental import pallas as pl
from jax.experimental.pallas import tpu as pltpu
from jax.sharding import Mesh, PartitionSpec as P

SEQ = 128
step_size = 0.02
ema_decay = 0.9

XL, NY, XH, NZ, NC = 2, 4, 2, 8, 2
F32, BF16 = jnp.float32, jnp.bfloat16

COLS_A = 256
VMEM_LIMIT = 56 * 1024 * 1024


def swap(a, axis, bit=1):
    size = {"xl": XL, "y": NY, "xh": XH, "z": NZ, "c": NC}[axis]
    return lax.ppermute(a, axis, [(i, i ^ bit) for i in range(size)])


def shift(a, by):
    return lax.ppermute(a, "z", [(i, (i + by) % NZ) for i in range(NZ)])


def after(a, *others):
    return lax.optimization_barrier((a, others))[0]


def tie(*arrays):
    return lax.optimization_barrier(arrays)


def grad_kernel(where_ref, level_ref, acts_ref, cotan_ref, *refs):
    outs, scaled_ref = refs[:4], refs[4]
    half = scaled_ref.shape[1] // 2

    @pl.when(pl.program_id(0) == 0)
    def _():
        first = where_ref[0] == 0
        for seq in range(level_ref.shape[0]):
            rows = pl.ds(seq * SEQ, SEQ)
            level = level_ref[seq].astype(F32) * 0.25
            low, high = cotan_ref[rows, :half], cotan_ref[rows, half:]
            scaled_ref[rows, :half] = (jnp.where(first, low, high).astype(F32) * level).astype(BF16)
            scaled_ref[rows, half:] = (jnp.where(first, high, low).astype(F32) * level).astype(BF16)

    product = lax.dot_general(
        acts_ref[...], scaled_ref[...], (((0,), (0,)), ((), ())), preferred_element_type=F32
    ).astype(BF16)
    at = 0
    for out in outs:
        cols = out.shape[-1]
        out[...] = product[:, at : at + cols].reshape(out.shape)
        at += cols


def partial_grad(core, side, levels, acts, cotan):
    tokens, width = acts.shape
    kv = cotan.shape[1]
    rows = width // (XH * NZ)
    steps = 2
    outs, specs = [], []
    for cols in (COLS_A, kv // 2 - COLS_A) * 2:
        outs.append(jax.ShapeDtypeStruct((XH, NZ, rows, cols), BF16))
        specs.append(pl.BlockSpec((1, NZ // steps, rows, cols), lambda i, *_: (i // steps, i % steps, 0, 0)))

    def block(i, at, _):
        return 0, jnp.where(i < steps, 1 - at[1], at[1]) * steps + i % steps

    return pl.pallas_call(
        grad_kernel,
        grid_spec=pltpu.PrefetchScalarGridSpec(
            num_scalar_prefetch=2,
            grid=(XH * steps,),
            in_specs=[
                pl.BlockSpec((tokens, width // (XH * steps)), block),
                pl.BlockSpec((tokens, kv), lambda i, *_: (0, 0)),
            ],
            out_specs=specs,
            scratch_shapes=[pltpu.VMEM((tokens, kv), BF16)],
        ),
        out_shape=outs,
        compiler_params=pltpu.CompilerParams(vmem_limit_bytes=VMEM_LIMIT),
        cost_estimate=pl.CostEstimate(
            flops=2 * tokens * width * kv,
            bytes_accessed=2 * (tokens * width + tokens * kv + width * kv),
            transcendentals=0,
        ),
        name="partial_grad",
    )(jnp.stack([core, side]).astype(jnp.int32), levels, acts, cotan)


def out_kernel(where_ref, own_ref, other_ref, *refs, slots):
    chunks, (out_own, out_other, whole, sems) = refs[: len(slots)], refs[len(slots) :]
    rows = whole.shape[0] // (XH * NZ)
    step = pl.program_id(0)
    depth = own_ref.shape[1]

    @pl.when(step == 0)
    def _():
        copies = []
        for ref, (col, places) in zip(chunks, slots):
            for src, row, size in places:
                index = len(copies)
                at = where_ref[index] * rows + row
                copies.append(
                    pltpu.make_async_copy(
                        ref.at[src],
                        whole.at[pl.ds(pl.multiple_of(at, 16), size), pl.ds(col, ref.shape[-1])],
                        sems.at[index],
                    )
                )
        for copy in copies:
            copy.start()
        for copy in copies:
            copy.wait()
        out_own[...] = jnp.zeros_like(out_own)
        out_other[...] = jnp.zeros_like(out_other)

    merged = whole[pl.ds(pl.multiple_of(step * depth, depth), depth), :]
    out_other[...] += jnp.dot(other_ref[...], merged, preferred_element_type=F32)
    out_own[...] += jnp.dot(own_ref[...], merged, preferred_element_type=F32)


def project(acts, acts_other, chunks, slots, where, cols):
    tokens, width = acts.shape
    steps = 4
    count = where.shape[0] - 1
    a_spec = pl.BlockSpec((tokens, width // steps), lambda i, *_: (0, i))
    own_spec = pl.BlockSpec((tokens, cols), lambda i, at: (0, at[count]))
    other_spec = pl.BlockSpec((tokens, cols), lambda i, *_: (0, 0))
    return pl.pallas_call(
        functools.partial(out_kernel, slots=slots),
        grid_spec=pltpu.PrefetchScalarGridSpec(
            num_scalar_prefetch=1,
            grid=(steps,),
            in_specs=[a_spec, a_spec] + [pl.BlockSpec(memory_space=pl.ANY)] * len(chunks),
            out_specs=[own_spec, other_spec],
            scratch_shapes=[pltpu.VMEM((width, cols), BF16), pltpu.SemaphoreType.DMA((count,))],
        ),
        out_shape=[
            jax.ShapeDtypeStruct((tokens, NC * cols), F32),
            jax.ShapeDtypeStruct((tokens, cols), F32),
        ],
        compiler_params=pltpu.CompilerParams(vmem_limit_bytes=VMEM_LIMIT),
        cost_estimate=pl.CostEstimate(
            flops=4 * tokens * width * cols,
            bytes_accessed=4 * tokens * width + 2 * width * cols + 8 * tokens * cols,
            transcendentals=0,
        ),
        name="project",
    )(where, acts, acts_other, *chunks)


def place_kernel(at_ref, columns_ref, _, out_ref, sem):
    cols = columns_ref.shape[1]
    start = pl.multiple_of(at_ref[0] * cols, cols)
    copy = pltpu.make_async_copy(columns_ref, out_ref.at[:, pl.ds(start, cols)], sem)
    copy.start()
    copy.wait()


def place_columns(at, columns, whole):
    return pl.pallas_call(
        place_kernel,
        grid_spec=pltpu.PrefetchScalarGridSpec(
            num_scalar_prefetch=1,
            grid=(1,),
            in_specs=[pl.BlockSpec(memory_space=pl.ANY)] * 2,
            out_specs=pl.BlockSpec(memory_space=pl.ANY),
            scratch_shapes=[pltpu.SemaphoreType.DMA],
        ),
        out_shape=jax.ShapeDtypeStruct(whole.shape, F32),
        input_output_aliases={2: 0},
        cost_estimate=pl.CostEstimate(flops=0, bytes_accessed=8 * columns.size, transcendentals=0),
        name="place_columns",
    )(at, columns, whole)


def on_device(acts, cotan, advantage, merge_ratio, weight, anchor, init):
    acts, cotan, levels, weight, anchor = acts[0], cotan[0], advantage[0], weight[0], anchor[0]
    tokens, width = acts.shape
    kv = cotan.shape[1]
    half = kv // 2
    blocks = XH * NZ
    own_rows = width // (blocks * NC)
    rows = own_rows * NC
    total_tokens = tokens * blocks * NC
    core, z, xh = lax.axis_index("c"), lax.axis_index("z"), lax.axis_index("xh")
    policy = lax.axis_index("xl") * NY + lax.axis_index("y")

    def my_half(a):
        return lax.dynamic_slice_in_dim(a, core * half, half, axis=-1)

    def other_half(a):
        return lax.dynamic_slice_in_dim(a, (1 - core) * half, half, axis=-1)

    def both_rows(mine, theirs):
        return jnp.where(core == 0, jnp.concatenate([mine, theirs], -2), jnp.concatenate([theirs, mine], -2))

    def both_cols(mine, theirs):
        return jnp.where(core == 0, jnp.concatenate([mine, theirs], -1), jnp.concatenate([theirs, mine], -1))

    given = jnp.stack([weight, init])
    given_got = swap(other_half(given), "c")
    acts_other = swap(after(acts, given_got), "c")
    given = both_rows(my_half(given), given_got)
    weight_half, init_half = given[0].astype(F32), given[1].astype(F32)
    init_up, init_down = shift(given[1], 1), shift(given[1], -1)

    *own, other_a, other_b = partial_grad(core, xh, levels, acts, cotan)
    early = (acts_other, init_up, init_down)
    got = [swap(after(other_a, *early), "c"), swap(after(other_b, *early), "c")]
    init_near = jnp.stack([given[1], init_up, init_down])
    init_across = swap(init_near, "xh")
    streams = (0, 1)

    def pick(a, k, side, sides):
        cut = lax.dynamic_slice(a, (side, (z + k + NZ) % NZ, 0, 0), (sides, 1, rows, a.shape[-1]))
        return cut.reshape(sides, rows, -1).astype(F32)

    def term(s, k, side=0, sides=2):
        return pick(own[s], k, side, sides) + pick(got[s], k, side, sides)

    zero = ((0, 0), (0, 0))
    cut = rows // 2
    down, up, sums = [None, None], [None, None], [None, None]
    last = ()
    ahead = {(3, 1): (init_across,)}
    for k in (4, 3, 2, 1, 0):
        for s in streams:
            if k == 4:
                send_down, send_up = term(s, -4, 0, 1), term(s, 4, 1, 1)
                if s == 1:
                    send_down, send_up, *_ = tie(send_down, send_up, *last)
            else:
                down[s], up[s], *_ = tie(down[s], up[s], *last, *ahead.get((k, s), ()))
                from_up, from_down = down[s].astype(F32), up[s].astype(F32)
                if k == 3:
                    from_up = jnp.pad(from_up, ((0, 1), *zero))
                    from_down = jnp.pad(from_down, ((1, 0), *zero))
                if k == 0:
                    sums[s] = term(s, 0) + from_up + from_down
                    send_down = send_up = sums[s][0].astype(BF16)
                else:
                    send_down, send_up = term(s, -k) + from_up, term(s, k) + from_down
            send_down, send_up = send_down.astype(BF16), send_up.astype(BF16)
            last = (send_down, send_up)
            if (k, s) == (3, 0):
                init_far = jnp.stack([shift(after(init_up, *last), 1), shift(after(init_down, *last), -1)])
                init_far_across = swap(init_far, "xh")
                ahead[1, 0] = (init_far,)
                ahead[0, 0] = (init_far_across,)
            if k == 0:
                down[s] = swap(send_down, "xh")
            else:
                down[s], up[s] = shift(send_down, -1), shift(send_up, 1)

    ratio = merge_ratio.astype(F32)
    shares = ratio / jnp.sum(ratio)
    share = shares[policy]
    bounds = ((0, COLS_A), (COLS_A, half))
    grads, mixes, norm = [None, None], [None, None], 0.0
    for s in streams:
        low, high = bounds[s]
        grads[s] = sums[s][1] + down[s].astype(F32)
        updated = weight_half[:, low:high] - step_size * grads[s] / math.sqrt(total_tokens)
        task = updated - init_half[:, low:high]
        norm = norm + jnp.sum(task * task)
        mixes[s] = (share * updated).astype(BF16)
    norms = jnp.where(lax.broadcasted_iota(jnp.int32, (8, 128), 0) == policy, norm, 0.0)
    last = ()
    for axis, bit in (("xl", 1), ("y", 1), ("y", 2)):
        arrived = [swap(mixes[0], axis, bit), swap(mixes[1], axis, bit)]
        norms_got = swap(after(norms, mixes[1]), axis, bit)
        for s in streams:
            if s == 1:
                arrived[s], norms_got, *_ = tie(arrived[s], norms_got, mixes[0])
                norms = norms + norms_got
            mixes[s] = mixes[s].astype(F32) + arrived[s].astype(F32)
            if (axis, bit) != ("y", 2):
                mixes[s] = mixes[s].astype(BF16)
    mixed_sq = 0.0
    for s in streams:
        low, high = bounds[s]
        mixed = mixes[s] - init_half[:, low:high]
        mixed_sq = mixed_sq + jnp.sum(mixed * mixed)
    scalars = jnp.where(lax.broadcasted_iota(jnp.int32, (8, 128), 1) == 0, norms, mixed_sq)

    def add_over(scalars, axis, bit, *others):
        scalars = after(scalars, *others)
        return scalars + swap(scalars, axis, bit)

    blocks_sent = [m.astype(BF16) for m in mixes]
    across = [swap(a, "xh") for a in blocks_sent]
    scalars = add_over(scalars, "z", 1, *blocks_sent)
    scalars = add_over(scalars, "z", 2)
    pairs = [jnp.stack([a, b]) for a, b in zip(blocks_sent, across)]
    up, down = [shift(pairs[0], 1), None], [shift(pairs[0], -1), None]
    pairs[1] = after(pairs[1], pairs[0])
    up[1], down[1] = shift(pairs[1], 1), shift(pairs[1], -1)
    far_scalars = swap(after(scalars, pairs[1]), "z", 4)

    def merge(k, mix, s):
        low, high = bounds[s]
        here, there = (init_far, init_far_across) if abs(k) == 2 else (init_near, init_across)
        at = {0: 0, -1: 1, 1: 2, -2: 0, 2: 1}[k]
        base = jnp.stack([here[at, :, low:high], there[at, :, low:high]]).astype(F32)
        return (base + (mix.astype(F32) - base) * factor).astype(BF16)

    def to_rows(a):
        mine = lax.dynamic_slice_in_dim(a, core * own_rows, own_rows, axis=0)
        theirs = lax.dynamic_slice_in_dim(a, (1 - core) * own_rows, own_rows, axis=0)
        return both_cols(mine, swap(theirs, "c"))

    grad_rows = to_rows(jnp.concatenate(grads, axis=1).astype(BF16)).astype(F32)
    anchor_new = ema_decay * anchor + (1.0 - ema_decay) * (
        weight.astype(F32) - step_size * grad_rows / math.sqrt(total_tokens)
    )

    chunks = [[], []]
    last = ()
    for k in (2, 3, 4):
        for s in streams:
            up[s], down[s], *_ = tie(up[s], down[s], *last)
            if k == 2 and s == 0:
                up[0], down[0], far_scalars = tie(up[0], down[0], far_scalars)
                scalars = add_over(scalars + far_scalars, "c", 1)
            if k == 2 and s == 1:
                scalars = add_over(scalars, "xh", 1, up[1])
                target = jnp.sum(shares * jnp.sqrt(scalars[:, 0]))
                factor = target / jnp.sqrt(scalars[0, 1])
            if k == 3 and s == 0:
                up[0], anchor_new = tie(up[0], anchor_new)
            if k == 3:
                up[s], down[s] = merge(-2, up[s], s), merge(2, down[s], s)
            chunks[s] += [(up[s], 1 - k), (down[s], k - 1)]
            if k == 4:
                up[s], down[s] = up[s][:, :cut], down[s][:, cut:]
            last = (up[s], down[s])
            up[s], down[s] = shift(up[s], 1), shift(down[s], -1)

    def place(x, k):
        return (x * NZ + (z + k + NZ) % NZ).astype(jnp.int32)

    arrays, slots, where, merged = [], [], [], []
    for s in streams:
        (up1, _), (down1, _), *rest = chunks[s]
        mine = merge(0, pairs[s], s)
        merged.append(mine[0])
        for array, k in [(mine, 0), (merge(-1, up1, s), -1), (merge(1, down1, s), 1)] + rest:
            arrays.append(array)
            slots.append((bounds[s][0], [(0, 0, rows), (1, 0, rows)]))
            where += [place(xh, k), place(1 - xh, k)]
        for array, row, size in ((up[s], 0, cut), (down[s], cut, rows - cut)):
            arrays.append(array)
            slots.append((bounds[s][0], [(0, row, size), (1, row, size)]))
            where += [place(xh, 4), place(1 - xh, 4)]
    merged_rows = to_rows(jnp.concatenate(merged, axis=1))
    here = core.astype(jnp.int32).reshape(1)
    where = jnp.concatenate([after(jnp.stack(where), merged_rows), here])
    mine, away = project(acts, acts_other, arrays, slots, where, half)
    result = place_columns(1 - here, swap(away, "c"), mine)

    return anchor_new[None], merged_rows, result[None]


def solution(mesh):
    mesh = Mesh(mesh.devices.reshape(XL, NY, XH, NZ, NC), ("xl", "y", "xh", "z", "c"))
    policy, zero = ("xl", "y"), ("xh", "z", "c")
    placed = (
        P(policy, zero, None),
        P(policy, zero, None),
        P(policy, zero),
        P(),
        P(policy, zero, None),
        P(policy, zero, None),
        P(zero, None),
    )
    return jax.shard_map(
        on_device,
        mesh=mesh,
        in_specs=placed,
        out_specs=(P(policy, zero, None), P(zero, None), P(policy, zero, None)),
        check_vma=False,
    )
```
